128 devices in a mesh: seq: 16 (over x_lo, z, core), fsdp: 8 (over y, x_hi).
Axes of the slice: x: 4 (x_hi: 2, x_lo: 2; x = x_hi * 2 + x_lo), y: 4, z: 4, core: 2. Of those that a mesh axis runs over, the one named last changes fastest.
Arguments:
- perturbed_codes: float32 [16, 1024, 2432], P('fsdp', 'seq'), may hold values from -6 to 6
- random_draws: float32 [2, 16, 1024, 2432], P(None, 'fsdp', 'seq'), may hold values from -6 to 6
- relative_rewards: float32 [16], P('fsdp'), may hold values from -4 to 4
- rescaling_gains: bfloat16 [2432], replicated, may hold values from 0.5 to 1.5
- triple_projector: bfloat16 [2432, 6144], P(None, 'seq'), may hold values from -2 to 2
- emission_projector: bfloat16 [2048, 2432], replicated, may hold values from -0.125 to 0.125
- payload_bypass_reducer: bfloat16 [2432, 32], replicated, may hold values from -0.125 to 0.125
- payload_bypass_lift: bfloat16 [32, 2048], replicated, may hold values from -1 to 1
- outlet_bypass_reducer: bfloat16 [2048, 32], replicated, may hold values from -0.125 to 0.125
- outlet_bypass_lift: bfloat16 [32, 2432], replicated, may hold values from -1 to 1
Outputs:
- ending_diffusion_image: float32 [16, 1024, 2432], P('fsdp', 'seq')
- grad_av: float32 [2432, 32], P(('seq', 'fsdp'))
- grad_bv: float32 [32, 2048], P(None, ('seq', 'fsdp'))
- outlet_reducer_derivative: float32 [2048, 32], P(('seq', 'fsdp'))
- output_up_gradient: float32 [32, 2432], P(None, ('seq', 'fsdp'))
The draws below stay inside these ranges and needn't reach their ends.
All inputs are finite; a program needn't handle non-finite values.
Results may differ from the reference program's by a relative error of at most 0.017.
Values may be sent and summed in bfloat16 or wider, within the bound.
A program may use at most 192 MiB of HBM per device.

```python
import math
import jax
import jax.numpy as jnp
from jax import lax

MODEL_WIDTH = 2432
FOCUS_BRANCHES = 32
BRANCH_SPAN = 64
BYPASS_INNER_DIM = 32
SEQ_LEN = 1024
SAMPLES = 16


def draw_triple_projector(key, part):
    key = jax.random.fold_in(key, 11)
    base = jax.random.truncated_normal(key, -4.0, 4.0, (MODEL_WIDTH, FOCUS_BRANCHES, 3, BRANCH_SPAN), jnp.float32) / math.sqrt(MODEL_WIDTH)
    return base.reshape(MODEL_WIDTH, 3 * FOCUS_BRANCHES * BRANCH_SPAN).astype(jnp.bfloat16)


def steps_of(stream_key, extent, split, smallest, largest):
    factor_of = 1.0
    for axis_at, shards_of in split:
        draws = jax.random.uniform(jax.random.fold_in(jax.random.fold_in(stream_key, 6), axis_at), (shards_of,), jnp.float32, smallest / len(split), largest / len(split))
        factor_of = factor_of * jnp.repeat(jnp.exp(draws), extent[axis_at] // shards_of).reshape((-1,) + (1,) * (len(extent) - 1 - axis_at))
    return factor_of


def centred(own_key, extent, scale, limit, shards=(), kind=jnp.bfloat16):
    result = scale * jax.random.normal(own_key, extent, jnp.float32)
    if shards:
        result = result * steps_of(own_key, extent, shards, -0.22, 0.18)
    return jnp.clip(result, -limit, limit).astype(kind)


def setup_inputs(seed: int = 0) -> dict:
    key_list = jax.random.split(jax.random.key(seed), 11)
    perturbed_codes = centred(key_list[0], (SAMPLES, SEQ_LEN, MODEL_WIDTH), 1.0, 6.0, ((0, 8), (1, 16)), jnp.float32)
    random_draws = centred(key_list[1], (2, SAMPLES, SEQ_LEN, MODEL_WIDTH), 1.0, 6.0, ((1, 8), (2, 16)), jnp.float32)
    relative_rewards = centred(key_list[2], (SAMPLES,), 1.0, 4.0, ((0, 8),), jnp.float32)
    rescaling_gains = jnp.clip(1.0 + 0.1 * jax.random.normal(key_list[3], (MODEL_WIDTH,), jnp.float32), 0.5, 1.5).astype(jnp.bfloat16)
    triple_projector = draw_triple_projector(jax.random.fold_in(key_list[10], 71), 0)
    emission_projector = centred(key_list[5], (FOCUS_BRANCHES * BRANCH_SPAN, MODEL_WIDTH), (FOCUS_BRANCHES * BRANCH_SPAN) ** -0.5, 0.125)
    payload_bypass_reducer = centred(key_list[6], (MODEL_WIDTH, BYPASS_INNER_DIM), MODEL_WIDTH ** -0.5, 0.125)
    payload_bypass_lift = centred(key_list[7], (BYPASS_INNER_DIM, FOCUS_BRANCHES * BRANCH_SPAN), BYPASS_INNER_DIM ** -0.5, 1.0)
    outlet_bypass_reducer = centred(key_list[8], (FOCUS_BRANCHES * BRANCH_SPAN, BYPASS_INNER_DIM), (FOCUS_BRANCHES * BRANCH_SPAN) ** -0.5, 0.125)
    outlet_bypass_lift = centred(key_list[9], (BYPASS_INNER_DIM, MODEL_WIDTH), BYPASS_INNER_DIM ** -0.5, 1.0)
    return dict(perturbed_codes=perturbed_codes, random_draws=random_draws, relative_rewards=relative_rewards, rescaling_gains=rescaling_gains, triple_projector=triple_projector, emission_projector=emission_projector, payload_bypass_reducer=payload_bypass_reducer, payload_bypass_lift=payload_bypass_lift, outlet_bypass_reducer=outlet_bypass_reducer, outlet_bypass_lift=outlet_bypass_lift)


TIMES = (0.8, 0.7)
STEP = -0.1
LEVEL = 0.7
EPS = 1e-06

def plan(index):
    moment = TIMES[index]
    sigma = LEVEL * math.sqrt(moment / (1.0 - moment))
    drift = sigma * sigma / (2.0 * moment)
    spread = sigma * math.sqrt(-STEP)
    keep = 1.0 + STEP * drift
    push = STEP * (1.0 + drift * (1.0 - moment))
    return (keep, push, spread)

def normed(current_iterate, rescaling_gains):
    power = lax.optimization_barrier(jnp.mean(current_iterate * current_iterate, axis=-1, keepdims=True))
    return (current_iterate * lax.rsqrt(power + EPS) * rescaling_gains.astype(jnp.float32)).astype(jnp.bfloat16)

def solitary_instance(current_iterate, paired_draws, cohort_relative_reward, rescaling_gains, triple_projector, emission_projector, payload_bypass_reducer, payload_bypass_lift, outlet_bypass_reducer, outlet_bypass_lift):
    draw_tally = current_iterate.shape[0]
    scale = BRANCH_SPAN ** (-0.5)
    accumulated_sums = [jnp.zeros(payload_bypass_reducer.shape, jnp.float32), jnp.zeros(payload_bypass_lift.shape, jnp.float32), jnp.zeros(outlet_bypass_reducer.shape, jnp.float32), jnp.zeros(outlet_bypass_lift.shape, jnp.float32)]
    for index in range(2):
        keep, push, spread = plan(index)
        hidden_rows = normed(current_iterate, rescaling_gains)
        payload_thin_lines = jnp.dot(hidden_rows, payload_bypass_reducer, preferred_element_type=jnp.float32).astype(jnp.bfloat16)
        mixed = jnp.dot(hidden_rows, triple_projector, preferred_element_type=jnp.float32).reshape(draw_tally, FOCUS_BRANCHES, 3, BRANCH_SPAN)
        iterate_increment = jnp.dot(payload_thin_lines, payload_bypass_lift, preferred_element_type=jnp.float32).reshape(draw_tally, FOCUS_BRANCHES, BRANCH_SPAN)
        mixed = mixed.at[:, :, 2, :].add(iterate_increment).astype(jnp.bfloat16).astype(jnp.float32)
        scores = jnp.einsum('qhe,khe->hqk', mixed[:, :, 0, :], mixed[:, :, 1, :]) * scale
        probs = jax.nn.softmax(scores, axis=-1).astype(jnp.bfloat16)
        blended_lookup_answer = jnp.einsum('hqk,khe->qhe', probs.astype(jnp.float32), mixed[:, :, 2, :])
        blended_lookup_answer = blended_lookup_answer.astype(jnp.bfloat16).reshape(draw_tally, FOCUS_BRANCHES * BRANCH_SPAN)
        outlet_thin_operand = jnp.dot(blended_lookup_answer, outlet_bypass_reducer, preferred_element_type=jnp.float32).astype(jnp.bfloat16)
        predicted_velocity = jnp.dot(blended_lookup_answer, emission_projector, preferred_element_type=jnp.float32) + jnp.dot(outlet_thin_operand, outlet_bypass_lift, preferred_element_type=jnp.float32)
        coef = -push / (2.0 * SAMPLES * spread)
        drift_field_derivative = (coef * cohort_relative_reward * paired_draws[index]).astype(jnp.bfloat16)
        accumulated_sums[3] = accumulated_sums[3] + jnp.dot(outlet_thin_operand.T, drift_field_derivative, preferred_element_type=jnp.float32)
        emitted_thin_derivative = jnp.dot(drift_field_derivative, outlet_bypass_lift.T, preferred_element_type=jnp.float32).astype(jnp.bfloat16)
        accumulated_sums[2] = accumulated_sums[2] + jnp.dot(blended_lookup_answer.T, emitted_thin_derivative, preferred_element_type=jnp.float32)
        emitted_derivative = (jnp.dot(drift_field_derivative, emission_projector.T, preferred_element_type=jnp.float32) + jnp.dot(emitted_thin_derivative, outlet_bypass_reducer.T, preferred_element_type=jnp.float32)).astype(jnp.bfloat16)
        payload_derivative_lines = jnp.einsum('hqk,qhe->khe', probs.astype(jnp.float32), emitted_derivative.reshape(draw_tally, FOCUS_BRANCHES, BRANCH_SPAN).astype(jnp.float32))
        payload_derivative_lines = payload_derivative_lines.astype(jnp.bfloat16).reshape(draw_tally, FOCUS_BRANCHES * BRANCH_SPAN)
        accumulated_sums[1] = accumulated_sums[1] + jnp.dot(payload_thin_lines.T, payload_derivative_lines, preferred_element_type=jnp.float32)
        payload_thin_derivative = jnp.dot(payload_derivative_lines, payload_bypass_lift.T, preferred_element_type=jnp.float32).astype(jnp.bfloat16)
        accumulated_sums[0] = accumulated_sums[0] + jnp.dot(hidden_rows.T, payload_thin_derivative, preferred_element_type=jnp.float32)
        current_iterate = keep * current_iterate + push * predicted_velocity + spread * paired_draws[index]
    return (current_iterate, accumulated_sums)

def reference(perturbed_codes, random_draws, relative_rewards, rescaling_gains, triple_projector, emission_projector, payload_bypass_reducer, payload_bypass_lift, outlet_bypass_reducer, outlet_bypass_lift):
    noise_by_sample = jnp.swapaxes(random_draws, 0, 1)

    def visit(carry, inputs):
        current_iterate, paired_draws, cohort_relative_reward = inputs
        closing_iterate, accumulated_sums = solitary_instance(current_iterate, paired_draws, cohort_relative_reward, rescaling_gains, triple_projector, emission_projector, payload_bypass_reducer, payload_bypass_lift, outlet_bypass_reducer, outlet_bypass_lift)
        carry = tuple((c + t for c, t in zip(carry, accumulated_sums)))
        return (carry, closing_iterate)
    opening_displacement = (jnp.zeros(payload_bypass_reducer.shape, jnp.float32), jnp.zeros(payload_bypass_lift.shape, jnp.float32), jnp.zeros(outlet_bypass_reducer.shape, jnp.float32), jnp.zeros(outlet_bypass_lift.shape, jnp.float32))
    sums, finals = lax.scan(visit, opening_displacement, (perturbed_codes, noise_by_sample, relative_rewards))
    return (finals, sums[0], sums[1], sums[2], sums[3])
```

```python
import functools
import math

import jax
import jax.numpy as jnp
from jax import lax
from jax.experimental import pallas as pl
from jax.experimental.pallas import tpu as pltpu
from jax.sharding import PartitionSpec as P

TIMES = (0.8, 0.7)
STEP = -0.1
LEVEL = 0.7
EPS = 1e-06
SAMPLES = 16
WIDTH = 2432
INNER = 2048
RANK = 32
F32 = jnp.float32
BF16 = jnp.bfloat16
MESH = pl.DeviceIdType.MESH
NT = (((1,), (1,)), ((), ()))


def plan(index):
    moment = TIMES[index]
    sigma = LEVEL * math.sqrt(moment / (1.0 - moment))
    drift = sigma * sigma / (2.0 * moment)
    spread = sigma * math.sqrt(-STEP)
    keep = 1.0 + STEP * drift
    push = STEP * (1.0 + drift * (1.0 - moment))
    return (keep, push, spread)


def mm(a, b):
    return jnp.dot(a, b, preferred_element_type=F32)


def mm_nt(a, b):
    return lax.dot_general(a, b, NT, preferred_element_type=F32)


def remote(src, dst, send, recv, device):
    return pltpu.make_async_remote_copy(
        src_ref=src,
        dst_ref=dst,
        send_sem=send,
        recv_sem=recv,
        device_id=device,
        device_id_type=MESH,
    )


def block_kernel(
    x0, draws, rewards, gains, w_in, e_hbm, vred, vlift, ored, olift,
    x_out, r1_out, r2_out,
    wall, ep, hid, q, kv, lowvt, dout, dsend, dlo, dlo_src, redp, lift2,
    att, att_src, dvel, vt, dv, dlv, dl_src, dl_in, gav, gup,
    hs, hr, ks, kr, ds_, dr, ls, lr, as_, ar, ts, tr, ws, wr, es,
):
    me = lax.axis_index("seq")
    fs = lax.axis_index("fsdp")
    x_lo, z, c = me // 8, (me // 2) % 4, me % 2
    y, x_hi = fs // 2, fs % 2
    group = z * 2 + c
    zp, zm, zo = (z + 1) % 4, (z + 3) % 4, (z + 2) % 4
    pending = []

    def col(zz, cc):
        return {"seq": (x_lo * 4 + zz) * 2 + cc, "fsdp": fs}

    def x_neighbour(step):
        xx = (x_hi * 2 + x_lo + step) % 4
        return {"seq": ((xx % 2) * 4 + z) * 2 + c, "fsdp": y * 2 + xx // 2}

    sibling = col(z, 1 - c)
    partner = {"seq": (me + 8) % 16, "fsdp": fs}

    def send(src, dst, s, r, device):
        copy = remote(src, dst, s, r, device)
        copy.start()
        pending.append(copy)

    def arrived(region, s, r):
        remote(region, region, s, r, sibling).wait_recv()

    loads = []
    for g in range(8):
        for h in range(2):
            copy = pltpu.make_async_copy(
                e_hbm.at[pl.ds(128 * (8 * h + g), 128), :],
                ep.at[pl.ds(256 * g + 128 * h, 128), :],
                es.at[2 * g + h],
            )
            copy.start()
            loads.append(copy)

    barrier = pltpu.get_barrier_semaphore()
    for d in range(1, 16):
        pl.semaphore_signal(
            barrier, inc=1, device_id={"seq": (me + d) % 16, "fsdp": fs}, device_id_type=MESH
        )
    outer = x_neighbour(jnp.where(x_lo == 0, -1, 1) + 4)
    pl.semaphore_signal(barrier, inc=1, device_id=outer, device_id_type=MESH)

    low_half = lax.broadcasted_iota(jnp.int32, (128, 128), 1) < 64

    own_w = pl.multiple_of(x_lo * 384, 128)

    def permute(i, _):
        rows = pl.ds(pl.multiple_of(i * 128, 128), 128)
        t0 = w_in[rows, 0:128].astype(F32)
        t1 = w_in[rows, 128:256].astype(F32)
        t2 = w_in[rows, 256:384].astype(F32)
        keys = pltpu.roll(jnp.where(low_half, t2, t0), 64, 1)
        wall[rows, pl.ds(own_w, 128)] = jnp.where(low_half, t0, t1).astype(BF16)
        wall[rows, pl.ds(own_w + 128, 128)] = keys.astype(BF16)
        wall[rows, pl.ds(own_w + 256, 128)] = jnp.where(low_half, t1, t2).astype(BF16)
        return 0

    lax.fori_loop(0, WIDTH // 128, permute, 0)

    def hid_rows(k, s, zz, cc, start=0, size=64):
        return hid.at[k, s, pl.ds(pl.multiple_of(64 * (2 * zz + cc) + start, 32), size), :]

    own_rows = pl.ds(pl.multiple_of(64 * group, 64), 64)

    def norm(k, s, x):
        power = jnp.mean(x * x, axis=-1, keepdims=True)
        h = (x * lax.rsqrt(power + EPS) * gains[...].astype(F32)).astype(BF16)
        hid[k, s, own_rows, :] = h

    def gather_start(k, s):
        p = 2 * k + s
        own = hid_rows(k, s, z, c)
        send(own, own, hs.at[p, 1], hr.at[p, 1], col(zp, c))
        send(own, own, hs.at[p, 2], hr.at[p, 2], col(zm, c))
        send(own, own, hs.at[p, 0], hr.at[p, 0], sibling)

    def gather_near(k, s):
        p = 2 * k + s
        below, above = hid_rows(k, s, zm, c), hid_rows(k, s, zp, c)
        arrived(below, hs.at[p, 1], hr.at[p, 1])
        half = hid_rows(k, s, zm, c, 0, 32)
        send(half, half, hs.at[p, 4], hr.at[p, 4], col(zp, c))
        send(below, below, hs.at[p, 3], hr.at[p, 3], sibling)
        arrived(above, hs.at[p, 2], hr.at[p, 2])
        half = hid_rows(k, s, zp, c, 32, 32)
        send(half, half, hs.at[p, 6], hr.at[p, 6], col(zm, c))
        send(above, above, hs.at[p, 5], hr.at[p, 5], sibling)

    def gather_far(k, s):
        p = 2 * k + s
        for n, start in ((4, 0), (6, 32)):
            half = hid_rows(k, s, zo, c, start, 32)
            arrived(half, hs.at[p, n], hr.at[p, n])
            m = 7 if n == 4 else 8
            send(half, half, hs.at[p, m], hr.at[p, m], sibling)

    def project(k, s, j):
        p = 2 * k + s
        zz = (z, zm, zp, zo)[j]
        if j == 0:
            arrived(hid_rows(k, s, z, 1 - c), hs.at[p, 0], hr.at[p, 0])
        elif j == 1:
            arrived(hid_rows(k, s, zm, 1 - c), hs.at[p, 3], hr.at[p, 3])
        elif j == 2:
            arrived(hid_rows(k, s, zp, 1 - c), hs.at[p, 5], hr.at[p, 5])
        else:
            arrived(hid_rows(k, s, zo, 1 - c, 0, 32), hs.at[p, 7], hr.at[p, 7])
            arrived(hid_rows(k, s, zo, 1 - c, 32, 32), hs.at[p, 8], hr.at[p, 8])
        base = pl.multiple_of(128 * zz, 128)
        rows = pl.ds(base, 128)
        there = pl.ds(pl.multiple_of(x_lo * 512 + 128 * zz, 128), 128)
        h = hid[k, s, rows, :]
        low = mm(h, vred[...])
        lowvt[k, s, x_lo, :, rows] = low.T.astype(BF16)
        add = mm(low.astype(BF16), lift2[...])
        mixed = mm(h, wall[...])
        q[s, rows, 0:128] = mixed[:, 0:128].astype(BF16)
        q[s, rows, 128:256] = mixed[:, 384:512].astype(BF16)
        kv[k, s, there, 0:128] = mixed[:, 128:256].astype(BF16)
        kv[k, s, there, 128:256] = (mixed[:, 256:384] + add[:, 0:128]).astype(BF16)
        kv[k, s, there, 256:384] = mixed[:, 512:640].astype(BF16)
        kv[k, s, there, 384:512] = (mixed[:, 640:768] + add[:, 128:256]).astype(BF16)
        region = kv.at[k, s, there, :]
        send(region, region, ks.at[p, j], kr.at[p, j], partner)
        if j == 3:
            region = lowvt.at[k, s, x_lo]
            send(region, region, ks.at[p, 4], kr.at[p, 4], partner)

    def attention(k, s):
        p = 2 * k + s
        for j in range(4):
            zz = (z, zm, zp, zo)[j]
            there = pl.ds(pl.multiple_of((1 - x_lo) * 512 + 128 * zz, 128), 128)
            arrived(kv.at[k, s, there, :], ks.at[p, j], kr.at[p, j])
        arrived(lowvt.at[k, s, 1 - x_lo], ks.at[p, 4], kr.at[p, 4])
        for n in range(2):
            vt[n] = kv[k, s, :, 256 * n + 128:256 * n + 256].astype(F32).T.astype(BF16)
        dv[...] = jnp.zeros_like(dv)
        head_of = lax.broadcasted_iota(jnp.int32, (256, 128), 1) < 64

        def tile(i, _):
            n, t = i // 2, i % 2
            rows = pl.ds(pl.multiple_of(t * 256, 256), 256)
            lanes = pl.ds(pl.multiple_of(n * 128, 128), 128)
            q2 = q[s, rows, lanes].astype(F32) * 0.125
            do2 = dout[p, rows, lanes].astype(F32)
            k2 = kv[k, s, :, pl.ds(pl.multiple_of(n * 256, 128), 128)]
            outs = []
            total = None
            for h in range(2):
                mask = head_of if h == 0 else jnp.logical_not(head_of)
                st = mm_nt(k2, jnp.where(mask, q2, 0.0).astype(BF16))
                e = jnp.exp(st - jnp.max(st, axis=0, keepdims=True))
                probs = (e * (1.0 / jnp.sum(e, axis=0, keepdims=True))).astype(BF16)
                outs.append(mm(vt[n, 64 * h:64 * h + 64, :], probs))
                term = mm(probs, jnp.where(mask, do2, 0.0).astype(BF16))
                total = term if total is None else total + term
            dv[:, lanes] += total
            att_src[k, s, rows, lanes] = jnp.concatenate(outs, axis=0).T.astype(BF16)
            return 0

        lax.fori_loop(0, 4, tile, 0)
        mine = pl.ds(pl.multiple_of(256 * group, 256), 256)
        for d in range(1, 8):
            g = (group + d) % 8
            send(
                att_src.at[k, s, pl.ds(pl.multiple_of(64 * g, 64), 64), :],
                att.at[k, s, :, mine],
                as_.at[p, d],
                ar.at[p, d],
                {"seq": x_lo * 8 + g, "fsdp": fs},
            )
        att[k, s, :, mine] = att_src[k, s, own_rows, :]

    def values_gradient(k, s):
        dvb = dv[...].astype(BF16)
        r2_out[0:32, :] += mm(lowvt[k, s, 0], dvb[0:512]) + mm(lowvt[k, s, 1], dvb[512:1024])
        dlv[s] = mm_nt(lift2[...], dvb)

    def send_low_values(k):
        lower = lax.broadcasted_iota(jnp.int32, (32, 128), 1) < 64
        for j in range(8):
            b0, b1 = dlv[0, :, 128 * j:128 * j + 128], dlv[1, :, 128 * j:128 * j + 128]
            dl_src[k, 2 * j] = jnp.where(lower, b0, pltpu.roll(b1, 64, 1))
            dl_src[k, 2 * j + 1] = jnp.where(lower, pltpu.roll(b0, 64, 1), b1)
        for d in range(1, 16):
            to = (me + d) % 16
            send(
                dl_src.at[k, to], dl_in.at[k, d], ts.at[k, d], tr.at[k, d], {"seq": to, "fsdp": fs}
            )

    def reducer_gradient(k):
        total = jnp.zeros((32, 256), F32)
        for g in range(8):
            both = jnp.concatenate(
                [att_src[k, 0, 64 * g:64 * g + 64, :], att_src[k, 1, 64 * g:64 * g + 64, :]], axis=0
            )
            total = total + mm(dlo[g, 32 * k:32 * k + 32, :], both)
        r2_out[32:64, :] += total

    def down_gradient(k):
        total = dl_src[k, me]
        for d in range(1, 16):
            arrived(dl_in.at[k, d], ts.at[k, d], tr.at[k, d])
            total = total + dl_in[k, d]
        both = jnp.concatenate([hid[k, 0, own_rows, :], hid[k, 1, own_rows, :]], axis=0)
        gav[...] += mm(total.astype(BF16), both)

    def outlet(k, s):
        p = 2 * k + s
        for d in range(1, 8):
            g = (group + 8 - d) % 8
            region = att.at[k, s, :, pl.ds(pl.multiple_of(256 * g, 256), 256)]
            arrived(region, as_.at[p, d], ar.at[p, d])
        keep, push, spread = plan(k)
        a = att[k, s]
        low = mm(a, redp[...])
        lowb = low.astype(BF16)
        rows = slice(128 * k + 64 * s, 128 * k + 64 * s + 64)
        gup[...] += mm(low.T.astype(BF16), dvel[rows, :])
        for start in range(0, WIDTH, 512):
            stop = min(start + 512, WIDTH)
            v = mm(a, ep[:, start:stop]) + mm(lowb, olift[:, start:stop])
            old = x0[s, :, start:stop] if k == 0 else x_out[s, :, start:stop]
            x_out[s, :, start:stop] = keep * old + push * v + spread * draws[k, s, :, start:stop]

    norm(0, 0, x0[0])
    norm(0, 1, x0[1])
    pl.semaphore_wait(barrier, 16)
    gather_start(0, 0)
    half = WIDTH // 2
    for n, step in ((0, 1), (1, 3)):
        region = wall.at[pl.ds(n * half, half), pl.ds(own_w, 384)]
        send(region, region, ws.at[n], wr.at[n], x_neighbour(step))
    gather_start(0, 1)

    lift2[:, 0:128] = vlift[:, pl.ds(pl.multiple_of(128 * group, 128), 128)]
    lift2[:, 128:256] = vlift[:, pl.ds(pl.multiple_of(1024 + 128 * group, 128), 128)]
    for g in range(8):
        for h in range(2):
            redp[256 * g + 128 * h:256 * g + 128 * h + 128, :] = ored[
                128 * (8 * h + g):128 * (8 * h + g) + 128, :
            ]
    r2_out[...] = jnp.zeros_like(r2_out)
    gav[...] = jnp.zeros_like(gav)
    gup[...] = jnp.zeros_like(gup)

    for k in range(2):
        keep, push, spread = plan(k)
        coef = -push / (2.0 * SAMPLES * spread)
        for s in range(2):
            start = 128 * k + 64 * s
            dvel[start:start + 64, :] = ((coef * rewards[s]) * draws[k, s]).astype(BF16)
    low = mm_nt(dvel[...], olift[...])
    lowb = low.astype(BF16)
    low_t = low.T.astype(BF16)
    for k in range(2):
        dlo_src[32 * k:32 * k + 32, :] = low_t[:, 128 * k:128 * k + 128]
    for d in range(1, 8):
        g = (group + d) % 8
        send(dlo_src, dlo.at[group], ls.at[d], lr.at[d], {"seq": x_lo * 8 + g, "fsdp": fs})
    dlo[group] = dlo_src[...]

    gather_near(0, 0)
    for copy in loads:
        copy.wait()

    def outlet_back(g, _):
        rows = pl.ds(pl.multiple_of(256 * g, 256), 256)
        d = mm_nt(dvel[...], ep[rows, :]) + mm_nt(lowb, redp[rows, :])
        dsend[g] = d.astype(BF16).reshape(4, 64, 256)
        return 0

    lax.fori_loop(0, 8, outlet_back, 0)
    gather_near(0, 1)
    gather_far(0, 0)
    for d in range(1, 8):
        g = (group + d) % 8
        send(
            dsend.at[g],
            dout.at[:, own_rows, :],
            ds_.at[d],
            dr.at[d],
            {"seq": x_lo * 8 + g, "fsdp": fs},
        )
    dout[:, own_rows, :] = dsend[group]
    gather_far(0, 1)
    for n in range(2):
        region = wall.at[pl.ds(n * half, half), pl.ds(pl.multiple_of((1 - x_lo) * 384, 128), 384)]
        arrived(region, ws.at[n], wr.at[n])

    for s in range(2):
        for j in range(4):
            project(0, s, j)
    for d in range(1, 8):
        g = (group + 8 - d) % 8
        rows = pl.ds(pl.multiple_of(64 * g, 64), 64)
        arrived(dout.at[:, rows, :], ds_.at[d], dr.at[d])
        arrived(dlo.at[g], ls.at[d], lr.at[d])

    attention(0, 0)
    values_gradient(0, 0)
    outlet(0, 0)
    norm(1, 0, x_out[0])
    gather_start(1, 0)
    attention(0, 1)
    gather_near(1, 0)
    values_gradient(0, 1)
    outlet(0, 1)
    norm(1, 1, x_out[1])
    gather_start(1, 1)
    gather_far(1, 0)
    for j in range(4):
        project(1, 0, j)
    gather_near(1, 1)
    send_low_values(0)
    reducer_gradient(0)
    gather_far(1, 1)
    for j in range(4):
        project(1, 1, j)
    attention(1, 0)
    values_gradient(1, 0)
    down_gradient(0)
    outlet(1, 0)
    attention(1, 1)
    values_gradient(1, 1)
    send_low_values(1)
    reducer_gradient(1)
    outlet(1, 1)
    down_gradient(1)
    r1_out[0:32, :] = gav[...]
    r1_out[32:64, :] = gup[...]
    for copy in pending:
        copy.wait_send()


def sum_kernel(a_ref, r_ref, out, a_in, r_in, b_src, b_in, s1, r1, s2, r2, s3, r3):
    me = lax.axis_index("seq")
    fs = lax.axis_index("fsdp")
    x_lo = me // 8
    pending = []
    barrier = pltpu.get_barrier_semaphore()
    for d in range(1, 16):
        pl.semaphore_signal(
            barrier, inc=1, device_id={"seq": (me + d) % 16, "fsdp": fs}, device_id_type=MESH
        )
    for d in range(1, 8):
        pl.semaphore_signal(
            barrier, inc=1, device_id={"seq": me, "fsdp": (fs + d) % 8}, device_id_type=MESH
        )
    pl.semaphore_wait(barrier, 22)

    def send(src, dst, s, r, device):
        copy = remote(src, dst, s, r, device)
        copy.start()
        pending.append(copy)
        return copy

    first = []
    for d in range(1, 16):
        to = (me + d) % 16
        first.append(
            send(a_ref.at[to], a_in.at[d], s1.at[d], r1.at[d], {"seq": to, "fsdp": fs})
        )
    other = send(
        r_ref.at[:, pl.ds(pl.multiple_of((1 - x_lo) * 128, 128), 128)],
        r_in, s2, r2, {"seq": (me + 8) % 16, "fsdp": fs},
    )
    other.wait_recv()
    b_src[:, 256:384] = r_ref[:, pl.ds(pl.multiple_of(x_lo * 128, 128), 128)] + r_in[...]
    total = a_ref[me]
    for d in range(1, 16):
        first[d - 1].wait_recv()
        total = total + a_in[d]
    b_src[:, 0:256] = total
    second = []
    for d in range(1, 8):
        second.append(
            send(b_src, b_in.at[d], s3.at[d], r3.at[d], {"seq": me, "fsdp": (fs + d) % 8})
        )
    total = b_src[...]
    for d in range(1, 8):
        second[d - 1].wait_recv()
        total = total + b_in[d]
    out[...] = total
    for copy in pending:
        copy.wait_send()


def per_device(
    perturbed_codes,
    random_draws,
    relative_rewards,
    rescaling_gains,
    triple_projector,
    emission_projector,
    payload_bypass_reducer,
    payload_bypass_lift,
    outlet_bypass_reducer,
    outlet_bypass_lift,
):
    vmem = pl.BlockSpec(memory_space=pltpu.VMEM)
    dma = pltpu.SemaphoreType.DMA
    final, r1, r2 = pl.pallas_call(
        block_kernel,
        out_shape=(
            jax.ShapeDtypeStruct((2, 64, WIDTH), F32),
            jax.ShapeDtypeStruct((64, WIDTH), F32),
            jax.ShapeDtypeStruct((64, 256), F32),
        ),
        in_specs=[
            vmem, vmem, pl.BlockSpec(memory_space=pltpu.SMEM), vmem, vmem,
            pl.BlockSpec(memory_space=pl.ANY), vmem, vmem, vmem, vmem,
        ],
        out_specs=(vmem, vmem, vmem),
        scratch_shapes=[
            pltpu.VMEM((WIDTH, 768), BF16),
            pltpu.VMEM((INNER, WIDTH), BF16),
            pltpu.VMEM((2, 2, 512, WIDTH), BF16),
            pltpu.VMEM((2, 512, 256), BF16),
            pltpu.VMEM((2, 2, 1024, 512), BF16),
            pltpu.VMEM((2, 2, 2, RANK, 512), BF16),
            pltpu.VMEM((4, 512, 256), BF16),
            pltpu.VMEM((8, 4, 64, 256), BF16),
            pltpu.VMEM((8, 64, 128), BF16),
            pltpu.VMEM((64, 128), BF16),
            pltpu.VMEM((INNER, RANK), BF16),
            pltpu.VMEM((RANK, 256), BF16),
            pltpu.VMEM((2, 2, 64, INNER), BF16),
            pltpu.VMEM((2, 2, 512, 256), BF16),
            pltpu.VMEM((256, WIDTH), BF16),
            pltpu.VMEM((2, 128, 1024), BF16),
            pltpu.VMEM((1024, 256), F32),
            pltpu.VMEM((2, RANK, 1024), F32),
            pltpu.VMEM((2, 16, RANK, 128), F32),
            pltpu.VMEM((2, 16, RANK, 128), F32),
            pltpu.VMEM((RANK, WIDTH), F32),
            pltpu.VMEM((RANK, WIDTH), F32),
            dma((4, 9)), dma((4, 9)),
            dma((4, 5)), dma((4, 5)),
            dma((8,)), dma((8,)),
            dma((8,)), dma((8,)),
            dma((4, 8)), dma((4, 8)),
            dma((2, 16)), dma((2, 16)),
            dma((2,)), dma((2,)),
            dma((16,)),
        ],
        compiler_params=pltpu.CompilerParams(
            collective_id=0, has_side_effects=True, vmem_limit_bytes=58 * 1024 * 1024
        ),
        name="rollout",
    )(
        perturbed_codes,
        random_draws,
        relative_rewards,
        rescaling_gains.reshape(1, WIDTH),
        triple_projector,
        emission_projector,
        payload_bypass_reducer,
        payload_bypass_lift,
        outlet_bypass_reducer,
        outlet_bypass_lift,
    )
    pieces = jnp.pad(
        r1.reshape(64, 16, WIDTH // 16).transpose(1, 0, 2), ((0, 0), (0, 0), (0, 256 - WIDTH // 16))
    )
    sums = pl.pallas_call(
        sum_kernel,
        out_shape=jax.ShapeDtypeStruct((64, 384), F32),
        in_specs=[vmem, vmem],
        out_specs=vmem,
        scratch_shapes=[
            pltpu.VMEM((16, 64, 256), F32),
            pltpu.VMEM((64, 128), F32),
            pltpu.VMEM((64, 384), F32),
            pltpu.VMEM((8, 64, 384), F32),
            dma((16,)), dma((16,)),
            dma, dma,
            dma((8,)), dma((8,)),
        ],
        compiler_params=pltpu.CompilerParams(
            collective_id=1, has_side_effects=True, vmem_limit_bytes=32 * 1024 * 1024
        ),
        name="gradient_sums",
    )(pieces, r2)
    mine = lax.axis_index("fsdp")
    wide = lax.dynamic_slice(sums, (0, mine * 19), (64, 19))
    narrow = lax.dynamic_slice(sums, (0, 256 + mine * 16), (64, 16))
    return (final, wide[0:32].T, narrow[0:32], narrow[32:64].T, wide[32:64])


def solution(mesh):
    placed = (
        P("fsdp", "seq", None),
        P(None, "fsdp", "seq", None),
        P("fsdp"),
        P(),
        P(None, "seq"),
        P(),
        P(),
        P(),
        P(),
        P(),
    )
    return jax.shard_map(
        per_device,
        mesh=mesh,
        in_specs=placed,
        out_specs=(
            P("fsdp", "seq", None),
            P(("seq", "fsdp"), None),
            P(None, ("seq", "fsdp")),
            P(("seq", "fsdp"), None),
            P(None, ("seq", "fsdp")),
        ),
        check_vma=False,
    )
```

```python
import math

import jax
import jax.numpy as jnp
from jax import lax
from jax.experimental import pallas as pl
from jax.experimental.pallas import tpu as pltpu
from jax.sharding import PartitionSpec as P

TIMES = (0.8, 0.7)
STEP = -0.1
LEVEL = 0.7
EPS = 1e-06
SAMPLES = 16
WIDTH = 2432
INNER = 2048
RANK = 32
F32 = jnp.float32
BF16 = jnp.bfloat16
MESH = pl.DeviceIdType.MESH
NT = (((1,), (1,)), ((), ()))
TN = (((0,), (0,)), ((), ()))


def plan(index):
    moment = TIMES[index]
    sigma = LEVEL * math.sqrt(moment / (1.0 - moment))
    drift = sigma * sigma / (2.0 * moment)
    spread = sigma * math.sqrt(-STEP)
    keep = 1.0 + STEP * drift
    push = STEP * (1.0 + drift * (1.0 - moment))
    return (keep, push, spread)


def mm(a, b):
    return jnp.dot(a, b, preferred_element_type=F32)


def mm_nt(a, b):
    return lax.dot_general(a, b, NT, preferred_element_type=F32)


def mm_tn(a, b):
    return lax.dot_general(a, b, TN, preferred_element_type=F32)


def remote(src, dst, send, recv, device):
    return pltpu.make_async_remote_copy(
        src_ref=src,
        dst_ref=dst,
        send_sem=send,
        recv_sem=recv,
        device_id=device,
        device_id_type=MESH,
    )


def block_kernel(
    x_hbm, draws_hbm, rewards, gains, w_hbm, e_hbm, vred_t, vlift, ored_t, olift,
    x_out, sums_out,
    x0, draws, w_in, r2_sum, a_src, a_in, r_in, b_src, b_in,
    wall, ep, hid, q, kv, lowvt, dout, dsend, dlo, dlo_src, redp, lift2,
    att, att_src, dvel, dv, dlv, dl_src, dl_in, gav, gup,
    hs, hr, ks, kr, ds_, dr, ls, lr, as_, ar, ts, tr, ws, wr, es,
    s1, t1, s2, t2, s3, t3, ins,
):
    me = lax.axis_index("seq")
    fs = lax.axis_index("fsdp")
    x_lo, z, c = me // 8, (me // 2) % 4, me % 2
    y, x_hi = fs // 2, fs % 2
    group = z * 2 + c
    zp, zm, zo = (z + 1) % 4, (z + 3) % 4, (z + 2) % 4
    pending = []

    def col(zz, cc):
        return {"seq": (x_lo * 4 + zz) * 2 + cc, "fsdp": fs}

    def x_neighbour(step):
        xx = (x_hi * 2 + x_lo + step) % 4
        return {"seq": ((xx % 2) * 4 + z) * 2 + c, "fsdp": y * 2 + xx // 2}

    sibling = col(z, 1 - c)
    partner = {"seq": (me + 8) % 16, "fsdp": fs}

    def send(src, dst, s, r, device):
        copy = remote(src, dst, s, r, device)
        copy.start()
        pending.append(copy)

    def arrived(region, s, r):
        remote(region, region, s, r, sibling).wait_recv()

    w_load = pltpu.make_async_copy(w_hbm, w_in, ins.at[0])
    x_load = pltpu.make_async_copy(x_hbm, x0, ins.at[1])
    draws_load = pltpu.make_async_copy(draws_hbm, draws, ins.at[2])
    w_load.start()
    x_load.start()
    draws_load.start()

    loads = []
    for g in range(8):
        for h in range(2):
            copy = pltpu.make_async_copy(
                e_hbm.at[pl.ds(128 * (8 * h + g), 128), :],
                ep.at[pl.ds(256 * g + 128 * h, 128), :],
                es.at[2 * g + h],
            )
            copy.start()
            loads.append(copy)

    barrier = pltpu.get_barrier_semaphore()
    for d in range(1, 16):
        pl.semaphore_signal(
            barrier, inc=1, device_id={"seq": (me + d) % 16, "fsdp": fs}, device_id_type=MESH
        )
    outer = x_neighbour(jnp.where(x_lo == 0, -1, 1) + 4)
    pl.semaphore_signal(barrier, inc=1, device_id=outer, device_id_type=MESH)
    for d in range(1, 8):
        pl.semaphore_signal(
            barrier, inc=1, device_id={"seq": me, "fsdp": (fs + d) % 8}, device_id_type=MESH
        )

    low_half = lax.broadcasted_iota(jnp.int32, (128, 128), 1) < 64

    own_w = pl.multiple_of(x_lo * 384, 128)

    def permute(i, _):
        rows = pl.ds(pl.multiple_of(i * 128, 128), 128)
        t0 = w_in[rows, 0:128].astype(F32)
        t1 = w_in[rows, 128:256].astype(F32)
        t2 = w_in[rows, 256:384].astype(F32)
        keys = pltpu.roll(jnp.where(low_half, t2, t0), 64, 1)
        wall[rows, pl.ds(own_w, 128)] = jnp.where(low_half, t0, t1).astype(BF16)
        wall[rows, pl.ds(own_w + 128, 128)] = keys.astype(BF16)
        wall[rows, pl.ds(own_w + 256, 128)] = jnp.where(low_half, t1, t2).astype(BF16)
        return 0

    w_load.wait()
    lax.fori_loop(0, WIDTH // 128, permute, 0)

    def hid_rows(k, s, zz, cc, start=0, size=64):
        return hid.at[k, s, pl.ds(pl.multiple_of(64 * (2 * zz + cc) + start, 32), size), :]

    own_rows = pl.ds(pl.multiple_of(64 * group, 64), 64)

    def norm(k, s, x):
        power = jnp.mean(x * x, axis=-1, keepdims=True)
        h = (x * lax.rsqrt(power + EPS) * gains[...].astype(F32)).astype(BF16)
        hid[k, s, own_rows, :] = h

    def gather_start(k, s):
        p = 2 * k + s
        own = hid_rows(k, s, z, c)
        send(own, own, hs.at[p, 1], hr.at[p, 1], col(zp, c))
        send(own, own, hs.at[p, 2], hr.at[p, 2], col(zm, c))
        send(own, own, hs.at[p, 0], hr.at[p, 0], sibling)

    def gather_near(k, s):
        p = 2 * k + s
        below, above = hid_rows(k, s, zm, c), hid_rows(k, s, zp, c)
        arrived(below, hs.at[p, 1], hr.at[p, 1])
        half = hid_rows(k, s, zm, c, 0, 32)
        send(half, half, hs.at[p, 4], hr.at[p, 4], col(zp, c))
        send(below, below, hs.at[p, 3], hr.at[p, 3], sibling)
        arrived(above, hs.at[p, 2], hr.at[p, 2])
        half = hid_rows(k, s, zp, c, 32, 32)
        send(half, half, hs.at[p, 6], hr.at[p, 6], col(zm, c))
        send(above, above, hs.at[p, 5], hr.at[p, 5], sibling)

    def gather_far(k, s):
        p = 2 * k + s
        for n, start in ((4, 0), (6, 32)):
            half = hid_rows(k, s, zo, c, start, 32)
            arrived(half, hs.at[p, n], hr.at[p, n])
            m = 7 if n == 4 else 8
            send(half, half, hs.at[p, m], hr.at[p, m], sibling)

    def project(k, s, j):
        p = 2 * k + s
        zz = (z, zm, zp, zo)[j]
        if j == 0:
            arrived(hid_rows(k, s, z, 1 - c), hs.at[p, 0], hr.at[p, 0])
        elif j == 1:
            arrived(hid_rows(k, s, zm, 1 - c), hs.at[p, 3], hr.at[p, 3])
        elif j == 2:
            arrived(hid_rows(k, s, zp, 1 - c), hs.at[p, 5], hr.at[p, 5])
        else:
            arrived(hid_rows(k, s, zo, 1 - c, 0, 32), hs.at[p, 7], hr.at[p, 7])
            arrived(hid_rows(k, s, zo, 1 - c, 32, 32), hs.at[p, 8], hr.at[p, 8])
        base = pl.multiple_of(128 * zz, 128)
        rows = pl.ds(base, 128)
        there = pl.ds(pl.multiple_of(x_lo * 512 + 128 * zz, 128), 128)
        h = hid[k, s, rows, :]
        low = mm_nt(h, vred_t[...])
        lowvt[k, s, x_lo, :, rows] = low.T.astype(BF16)
        add = mm(low.astype(BF16), lift2[...])
        mixed = mm(h, wall[...])
        q[s, rows, 0:128] = (mixed[:, 0:128] * 0.125).astype(BF16)
        q[s, rows, 128:256] = (mixed[:, 384:512] * 0.125).astype(BF16)
        kv[k, s, there, 0:128] = mixed[:, 128:256].astype(BF16)
        kv[k, s, there, 128:256] = (mixed[:, 256:384] + add[:, 0:128]).astype(BF16)
        kv[k, s, there, 256:384] = mixed[:, 512:640].astype(BF16)
        kv[k, s, there, 384:512] = (mixed[:, 640:768] + add[:, 128:256]).astype(BF16)
        region = kv.at[k, s, there, :]
        send(region, region, ks.at[p, j], kr.at[p, j], partner)
        if j == 3:
            region = lowvt.at[k, s, x_lo]
            send(region, region, ks.at[p, 4], kr.at[p, 4], partner)

    def attention(k, s):
        p = 2 * k + s
        for j in range(4):
            zz = (z, zm, zp, zo)[j]
            there = pl.ds(pl.multiple_of((1 - x_lo) * 512 + 128 * zz, 128), 128)
            arrived(kv.at[k, s, there, :], ks.at[p, j], kr.at[p, j])
        arrived(lowvt.at[k, s, 1 - x_lo], ks.at[p, 4], kr.at[p, 4])
        lower = lax.broadcasted_iota(jnp.int32, (512, 128), 1) < 64
        for n in range(2):
            lanes = slice(128 * n, 128 * n + 128)
            q2 = q[s, :, lanes].astype(F32)
            do2 = dout[p, :, lanes].astype(F32)
            k2 = kv[k, s, :, 256 * n:256 * n + 128]
            v2 = kv[k, s, :, 256 * n + 128:256 * n + 256]
            outs = []
            total = None
            for h in range(2):
                mask = lower if h == 0 else jnp.logical_not(lower)
                st = mm_nt(k2, jnp.where(mask, q2, 0.0).astype(BF16))
                e = jnp.exp(st - jnp.max(st, axis=0, keepdims=True))
                probs = (e * (1.0 / jnp.sum(e, axis=0, keepdims=True))).astype(BF16)
                outs.append(mm_tn(probs, v2))
                term = mm(probs, jnp.where(mask, do2, 0.0).astype(BF16))
                total = term if total is None else total + term
            dv[:, lanes] = total.astype(BF16)
            att_src[k, s, :, lanes] = jnp.where(lower, outs[0], outs[1]).astype(BF16)
        mine = pl.ds(pl.multiple_of(256 * group, 256), 256)
        for d in range(1, 8):
            g = (group + d) % 8
            send(
                att_src.at[k, s, pl.ds(pl.multiple_of(64 * g, 64), 64), :],
                att.at[k, s, :, mine],
                as_.at[p, d],
                ar.at[p, d],
                {"seq": x_lo * 8 + g, "fsdp": fs},
            )
        att[k, s, :, mine] = att_src[k, s, own_rows, :]

    def values_gradient(k, s):
        dvb = dv[...]
        r2_sum[0:32, :] += mm(lowvt[k, s, 0], dvb[0:512]) + mm(lowvt[k, s, 1], dvb[512:1024])
        dlv[s] = mm_nt(lift2[...], dvb)

    def send_low_values(k):
        lower = lax.broadcasted_iota(jnp.int32, (32, 128), 1) < 64
        for j in range(8):
            b0, b1 = dlv[0, :, 128 * j:128 * j + 128], dlv[1, :, 128 * j:128 * j + 128]
            dl_src[k, 2 * j] = jnp.where(lower, b0, pltpu.roll(b1, 64, 1))
            dl_src[k, 2 * j + 1] = jnp.where(lower, pltpu.roll(b0, 64, 1), b1)
        for d in range(1, 16):
            to = (me + d) % 16
            send(
                dl_src.at[k, to], dl_in.at[k, d], ts.at[k, d], tr.at[k, d], {"seq": to, "fsdp": fs}
            )

    def reducer_gradient(k):
        total = jnp.zeros((32, 256), F32)
        for g in range(8):
            both = jnp.concatenate(
                [att_src[k, 0, 64 * g:64 * g + 64, :], att_src[k, 1, 64 * g:64 * g + 64, :]], axis=0
            )
            total = total + mm(dlo[g, 32 * k:32 * k + 32, :], both)
        r2_sum[32:64, :] += total

    def down_gradient(k):
        total = dl_src[k, me]
        for d in range(1, 16):
            arrived(dl_in.at[k, d], ts.at[k, d], tr.at[k, d])
            total = total + dl_in[k, d]
        both = jnp.concatenate([hid[k, 0, own_rows, :], hid[k, 1, own_rows, :]], axis=0)
        gav[...] += mm(total.astype(BF16), both)

    def outlet(k, s):
        p = 2 * k + s
        for d in range(1, 8):
            g = (group + 8 - d) % 8
            region = att.at[k, s, :, pl.ds(pl.multiple_of(256 * g, 256), 256)]
            arrived(region, as_.at[p, d], ar.at[p, d])
        keep, push, spread = plan(k)
        a = att[k, s]
        low = mm_nt(a, redp[...])
        lowb = low.astype(BF16)
        rows = slice(128 * k + 64 * s, 128 * k + 64 * s + 64)
        gup[...] += mm(low.T.astype(BF16), dvel[rows, :])
        for start in range(0, WIDTH, 512):
            stop = min(start + 512, WIDTH)
            v = mm(a, ep[:, start:stop]) + mm(lowb, olift[:, start:stop])
            old = x0[s, :, start:stop] if k == 0 else x_out[s, :, start:stop]
            x_out[s, :, start:stop] = keep * old + push * v + spread * draws[k, s, :, start:stop]

    pl.semaphore_wait(barrier, 23)
    half = WIDTH // 2
    for n, step in ((0, 1), (1, 3)):
        region = wall.at[pl.ds(n * half, half), pl.ds(own_w, 384)]
        send(region, region, ws.at[n], wr.at[n], x_neighbour(step))
    x_load.wait()
    norm(0, 0, x0[0])
    gather_start(0, 0)
    norm(0, 1, x0[1])
    gather_start(0, 1)
    draws_load.wait()

    lift2[:, 0:128] = vlift[:, pl.ds(pl.multiple_of(128 * group, 128), 128)]
    lift2[:, 128:256] = vlift[:, pl.ds(pl.multiple_of(1024 + 128 * group, 128), 128)]
    for g in range(8):
        for h in range(2):
            redp[:, 256 * g + 128 * h:256 * g + 128 * h + 128] = ored_t[
                :, 128 * (8 * h + g):128 * (8 * h + g) + 128
            ]
    r2_sum[...] = jnp.zeros_like(r2_sum)
    gav[...] = jnp.zeros_like(gav)
    gup[...] = jnp.zeros_like(gup)

    for k in range(2):
        keep, push, spread = plan(k)
        coef = -push / (2.0 * SAMPLES * spread)
        for s in range(2):
            start = 128 * k + 64 * s
            dvel[start:start + 64, :] = ((coef * rewards[s]) * draws[k, s]).astype(BF16)
    low = mm_nt(dvel[...], olift[...])
    lowb = low.astype(BF16)
    low_t = low.T.astype(BF16)
    for k in range(2):
        dlo_src[32 * k:32 * k + 32, :] = low_t[:, 128 * k:128 * k + 128]
    for d in range(1, 8):
        g = (group + d) % 8
        send(dlo_src, dlo.at[group], ls.at[d], lr.at[d], {"seq": x_lo * 8 + g, "fsdp": fs})
    dlo[group] = dlo_src[...]

    gather_near(0, 0)
    for copy in loads:
        copy.wait()

    def outlet_back(g, _):
        rows = pl.ds(pl.multiple_of(256 * g, 256), 256)
        d = mm_nt(dvel[...], ep[rows, :]) + mm(lowb, redp[:, rows])
        dsend[g] = d.astype(BF16).reshape(4, 64, 256)
        return 0

    lax.fori_loop(0, 8, outlet_back, 0)
    gather_near(0, 1)
    gather_far(0, 0)
    for d in range(1, 8):
        g = (group + d) % 8
        send(
            dsend.at[g],
            dout.at[:, own_rows, :],
            ds_.at[d],
            dr.at[d],
            {"seq": x_lo * 8 + g, "fsdp": fs},
        )
    dout[:, own_rows, :] = dsend[group]
    gather_far(0, 1)
    for n in range(2):
        region = wall.at[pl.ds(n * half, half), pl.ds(pl.multiple_of((1 - x_lo) * 384, 128), 384)]
        arrived(region, ws.at[n], wr.at[n])

    for s in range(2):
        for j in range(4):
            project(0, s, j)
    for d in range(1, 8):
        g = (group + 8 - d) % 8
        rows = pl.ds(pl.multiple_of(64 * g, 64), 64)
        arrived(dout.at[:, rows, :], ds_.at[d], dr.at[d])
        arrived(dlo.at[g], ls.at[d], lr.at[d])

    attention(0, 0)
    values_gradient(0, 0)
    outlet(0, 0)
    norm(1, 0, x_out[0])
    gather_start(1, 0)
    attention(0, 1)
    gather_near(1, 0)
    values_gradient(0, 1)
    send_low_values(0)
    gather_far(1, 0)
    for j in range(4):
        project(1, 0, j)
    outlet(0, 1)
    norm(1, 1, x_out[1])
    gather_start(1, 1)
    reducer_gradient(0)
    down_gradient(0)
    gather_near(1, 1)
    attention(1, 0)
    gather_far(1, 1)
    for j in range(4):
        project(1, 1, j)
    values_gradient(1, 0)
    outlet(1, 0)
    attention(1, 1)
    values_gradient(1, 1)
    send_low_values(1)
    reducer_gradient(1)
    send(
        r2_sum.at[:, pl.ds(pl.multiple_of((1 - x_lo) * 128, 128), 128)], r_in, s2, t2, partner
    )
    outlet(1, 1)
    down_gradient(1)

    part = WIDTH // 16
    for t in range(16):
        a_src[t] = jnp.concatenate(
            [
                gav[:, part * t:part * t + part],
                gup[:, part * t:part * t + part],
                jnp.zeros((RANK, 384 - 2 * part), F32),
            ],
            axis=1,
        ).astype(BF16)
    for d in range(1, 16):
        to = (me + d) % 16
        send(a_src.at[to], a_in.at[d], s1.at[d], t1.at[d], {"seq": to, "fsdp": fs})
    arrived(r_in, s2, t2)
    narrow = r2_sum[:, pl.ds(pl.multiple_of(x_lo * 128, 128), 128)] + r_in[...]
    total = a_src[me].astype(F32)
    for d in range(1, 16):
        arrived(a_in.at[d], s1.at[d], t1.at[d])
        total = total + a_in[d].astype(F32)

    step = part // 8
    for f in range(8):
        b_src[f] = jnp.concatenate(
            [
                total[:, step * f:step * f + step],
                total[:, part + step * f:part + step * f + step],
                narrow[0:32, 16 * f:16 * f + 16],
                narrow[32:64, 16 * f:16 * f + 16],
                jnp.zeros((RANK, 128 - 2 * step - 32), F32),
            ],
            axis=1,
        )
    for d in range(1, 8):
        to = (fs + d) % 8
        send(b_src.at[to], b_in.at[d], s3.at[d], t3.at[d], {"seq": me, "fsdp": to})
    total = b_src[fs]
    for d in range(1, 8):
        arrived(b_in.at[d], s3.at[d], t3.at[d])
        total = total + b_in[d]
    sums_out[...] = total.T
    for copy in pending:
        copy.wait_send()


def place_kernel(x_in, sums, x_out, gav, gup, gbv, gred, sem):
    copy = pltpu.make_async_copy(x_in, x_out, sem)
    copy.start()
    wide, narrow = gav.shape[0], gbv.shape[0]
    gav[...] = sums[0:wide, :]
    gup[...] = sums[wide:2 * wide, :]
    gbv[...] = sums[2 * wide:2 * wide + narrow, :]
    gred[...] = sums[2 * wide + narrow:2 * wide + 2 * narrow, :]
    copy.wait()


def per_device(
    perturbed_codes,
    random_draws,
    relative_rewards,
    rescaling_gains,
    triple_projector,
    emission_projector,
    payload_bypass_reducer,
    payload_bypass_lift,
    outlet_bypass_reducer,
    outlet_bypass_lift,
):
    vmem = pl.BlockSpec(memory_space=pltpu.VMEM)
    hbm = pl.BlockSpec(memory_space=pl.ANY)
    dma = pltpu.SemaphoreType.DMA
    final, sums = pl.pallas_call(
        block_kernel,
        out_shape=(
            jax.ShapeDtypeStruct((2, 64, WIDTH), F32),
            jax.ShapeDtypeStruct((128, RANK), F32),
        ),
        in_specs=[
            hbm, hbm, pl.BlockSpec(memory_space=pltpu.SMEM), vmem, hbm,
            hbm, vmem, vmem, vmem, vmem,
        ],
        out_specs=(vmem, vmem),
        scratch_shapes=[
            pltpu.VMEM((2, 64, WIDTH), F32),
            pltpu.VMEM((2, 2, 64, WIDTH), F32),
            pltpu.VMEM((WIDTH, 384), BF16),
            pltpu.VMEM((64, 256), F32),
            pltpu.VMEM((16, RANK, 384), BF16),
            pltpu.VMEM((16, RANK, 384), BF16),
            pltpu.VMEM((64, 128), F32),
            pltpu.VMEM((8, RANK, 128), F32),
            pltpu.VMEM((8, RANK, 128), F32),
            pltpu.VMEM((WIDTH, 768), BF16),
            pltpu.VMEM((INNER, WIDTH), BF16),
            pltpu.VMEM((2, 2, 512, WIDTH), BF16),
            pltpu.VMEM((2, 512, 256), BF16),
            pltpu.VMEM((2, 2, 1024, 512), BF16),
            pltpu.VMEM((2, 2, 2, RANK, 512), BF16),
            pltpu.VMEM((4, 512, 256), BF16),
            pltpu.VMEM((8, 4, 64, 256), BF16),
            pltpu.VMEM((8, 64, 128), BF16),
            pltpu.VMEM((64, 128), BF16),
            pltpu.VMEM((RANK, INNER), BF16),
            pltpu.VMEM((RANK, 256), BF16),
            pltpu.VMEM((2, 2, 64, INNER), BF16),
            pltpu.VMEM((2, 2, 512, 256), BF16),
            pltpu.VMEM((256, WIDTH), BF16),
            pltpu.VMEM((1024, 256), BF16),
            pltpu.VMEM((2, RANK, 1024), F32),
            pltpu.VMEM((2, 16, RANK, 128), F32),
            pltpu.VMEM((2, 16, RANK, 128), F32),
            pltpu.VMEM((RANK, WIDTH), F32),
            pltpu.VMEM((RANK, WIDTH), F32),
            dma((4, 9)), dma((4, 9)),
            dma((4, 5)), dma((4, 5)),
            dma((8,)), dma((8,)),
            dma((8,)), dma((8,)),
            dma((4, 8)), dma((4, 8)),
            dma((2, 16)), dma((2, 16)),
            dma((2,)), dma((2,)),
            dma((16,)),
            dma((16,)), dma((16,)),
            dma, dma,
            dma((8,)), dma((8,)),
            dma((3,)),
        ],
        compiler_params=pltpu.CompilerParams(
            collective_id=0, has_side_effects=True, vmem_limit_bytes=58 * 1024 * 1024
        ),
        name="rollout",
    )(
        perturbed_codes,
        random_draws,
        relative_rewards,
        rescaling_gains.reshape(1, WIDTH),
        triple_projector,
        emission_projector,
        payload_bypass_reducer.T,
        payload_bypass_lift,
        outlet_bypass_reducer.T,
        outlet_bypass_lift,
    )
    wide, narrow = WIDTH // 128, INNER // 128
    final, gav, gup, gbv, gred = pl.pallas_call(
        place_kernel,
        out_shape=(
            jax.ShapeDtypeStruct(final.shape, F32),
            jax.ShapeDtypeStruct((wide, RANK), F32),
            jax.ShapeDtypeStruct((wide, RANK), F32),
            jax.ShapeDtypeStruct((narrow, RANK), F32),
            jax.ShapeDtypeStruct((narrow, RANK), F32),
        ),
        in_specs=[hbm, vmem],
        out_specs=(hbm, vmem, vmem, vmem, vmem),
        scratch_shapes=[dma],
        name="place",
    )(final, sums)
    return (final, gav, gbv.T, gred, gup.T)


def solution(mesh):
    placed = (
        P("fsdp", "seq", None),
        P(None, "fsdp", "seq", None),
        P("fsdp"),
        P(),
        P(None, "seq"),
        P(),
        P(),
        P(),
        P(),
        P(),
    )
    return jax.shard_map(
        per_device,
        mesh=mesh,
        in_specs=placed,
        out_specs=(
            P("fsdp", "seq", None),
            P(("seq", "fsdp"), None),
            P(None, ("seq", "fsdp")),
            P(("seq", "fsdp"), None),
            P(None, ("seq", "fsdp")),
        ),
        check_vma=False,
    )
```

```python
import math

import jax
import jax.numpy as jnp
from jax import lax
from jax.experimental import pallas as pl
from jax.experimental.pallas import tpu as pltpu
from jax.sharding import PartitionSpec as P

TIMES = (0.8, 0.7)
STEP = -0.1
LEVEL = 0.7
EPS = 1e-06
SAMPLES = 16
WIDTH = 2432
INNER = 2048
RANK = 32
F32 = jnp.float32
BF16 = jnp.bfloat16
MESH = pl.DeviceIdType.MESH
NT = (((1,), (1,)), ((), ()))
TN = (((0,), (0,)), ((), ()))


def plan(index):
    moment = TIMES[index]
    sigma = LEVEL * math.sqrt(moment / (1.0 - moment))
    drift = sigma * sigma / (2.0 * moment)
    spread = sigma * math.sqrt(-STEP)
    keep = 1.0 + STEP * drift
    push = STEP * (1.0 + drift * (1.0 - moment))
    return (keep, push, spread)


def mm(a, b):
    return jnp.dot(a, b, preferred_element_type=F32)


def mm_nt(a, b):
    return lax.dot_general(a, b, NT, preferred_element_type=F32)


def mm_tn(a, b):
    return lax.dot_general(a, b, TN, preferred_element_type=F32)


def remote(src, dst, send, recv, device):
    return pltpu.make_async_remote_copy(
        src_ref=src,
        dst_ref=dst,
        send_sem=send,
        recv_sem=recv,
        device_id=device,
        device_id_type=MESH,
    )


def block_kernel(
    x_hbm, draws_hbm, rewards, gains, w_hbm, e_hbm, vred_t, vlift, ored_t, olift,
    x_out, sums_out,
    x0, draws, w_in, r2_sum, a_src, a_in, r_in, b_src, b_in,
    wall, ep, hid, q, kv, lowvt, dout, dsend, dlo, dlo_src, redp, lift2,
    att, att_src, dvel, dv, dlv, dl_src, dl_in, gav, gup,
    hs, hr, ks, kr, ds_, dr, ls, lr, as_, ar, ts, tr, ws, wr, es,
    s1, t1, s2, t2, s3, t3, ins,
):
    me = lax.axis_index("seq")
    fs = lax.axis_index("fsdp")
    x_lo, z, c = me // 8, (me // 2) % 4, me % 2
    y, x_hi = fs // 2, fs % 2
    group = z * 2 + c
    zp, zm, zo = (z + 1) % 4, (z + 3) % 4, (z + 2) % 4
    pending = []

    def col(zz, cc):
        return {"seq": (x_lo * 4 + zz) * 2 + cc, "fsdp": fs}

    def x_neighbour(step):
        xx = (x_hi * 2 + x_lo + step) % 4
        return {"seq": ((xx % 2) * 4 + z) * 2 + c, "fsdp": y * 2 + xx // 2}

    sibling = col(z, 1 - c)
    partner = {"seq": (me + 8) % 16, "fsdp": fs}

    def send(src, dst, s, r, device):
        copy = remote(src, dst, s, r, device)
        copy.start()
        pending.append(copy)

    def arrived(region, s, r):
        remote(region, region, s, r, sibling).wait_recv()

    w_load = pltpu.make_async_copy(w_hbm, w_in, ins.at[0])
    x_load = pltpu.make_async_copy(x_hbm, x0, ins.at[1])
    draws_load = pltpu.make_async_copy(draws_hbm, draws, ins.at[2])
    w_load.start()
    x_load.start()
    draws_load.start()

    loads = []
    for g in range(8):
        for h in range(2):
            copy = pltpu.make_async_copy(
                e_hbm.at[pl.ds(128 * (8 * h + g), 128), :],
                ep.at[pl.ds(256 * g + 128 * h, 128), :],
                es.at[2 * g + h],
            )
            copy.start()
            loads.append(copy)

    barrier = pltpu.get_barrier_semaphore()
    for d in range(1, 16):
        pl.semaphore_signal(
            barrier, inc=1, device_id={"seq": (me + d) % 16, "fsdp": fs}, device_id_type=MESH
        )
    outer = x_neighbour(jnp.where(x_lo == 0, -1, 1) + 4)
    pl.semaphore_signal(barrier, inc=1, device_id=outer, device_id_type=MESH)
    for d in range(1, 8):
        pl.semaphore_signal(
            barrier, inc=1, device_id={"seq": me, "fsdp": (fs + d) % 8}, device_id_type=MESH
        )

    low_half = lax.broadcasted_iota(jnp.int32, (128, 128), 1) < 64

    own_w = pl.multiple_of(x_lo * 384, 128)

    def permute(i, _):
        rows = pl.ds(pl.multiple_of(i * 128, 128), 128)
        t0 = w_in[rows, 0:128].astype(F32)
        t1 = w_in[rows, 128:256].astype(F32)
        t2 = w_in[rows, 256:384].astype(F32)
        keys = pltpu.roll(jnp.where(low_half, t2, t0), 64, 1)
        wall[rows, pl.ds(own_w, 128)] = jnp.where(low_half, t0, t1).astype(BF16)
        wall[rows, pl.ds(own_w + 128, 128)] = keys.astype(BF16)
        wall[rows, pl.ds(own_w + 256, 128)] = jnp.where(low_half, t1, t2).astype(BF16)
        return 0

    w_load.wait()
    lax.fori_loop(0, WIDTH // 128, permute, 0)

    def hid_rows(k, s, zz, cc, start=0, size=64):
        return hid.at[k, s, pl.ds(pl.multiple_of(64 * (2 * zz + cc) + start, 32), size), :]

    own_rows = pl.ds(pl.multiple_of(64 * group, 64), 64)

    def norm(k, s, x):
        power = jnp.mean(x * x, axis=-1, keepdims=True)
        h = (x * lax.rsqrt(power + EPS) * gains[...].astype(F32)).astype(BF16)
        hid[k, s, own_rows, :] = h

    def gather_start(k, s):
        p = 2 * k + s
        own = hid_rows(k, s, z, c)
        send(own, own, hs.at[p, 1], hr.at[p, 1], col(zp, c))
        send(own, own, hs.at[p, 2], hr.at[p, 2], col(zm, c))
        send(own, own, hs.at[p, 0], hr.at[p, 0], sibling)

    def gather_near(k, s):
        p = 2 * k + s
        below, above = hid_rows(k, s, zm, c), hid_rows(k, s, zp, c)
        arrived(below, hs.at[p, 1], hr.at[p, 1])
        half = hid_rows(k, s, zm, c, 0, 32)
        send(half, half, hs.at[p, 4], hr.at[p, 4], col(zp, c))
        send(below, below, hs.at[p, 3], hr.at[p, 3], sibling)
        arrived(above, hs.at[p, 2], hr.at[p, 2])
        half = hid_rows(k, s, zp, c, 32, 32)
        send(half, half, hs.at[p, 6], hr.at[p, 6], col(zm, c))
        send(above, above, hs.at[p, 5], hr.at[p, 5], sibling)

    def gather_far(k, s):
        p = 2 * k + s
        for n, start in ((4, 0), (6, 32)):
            half = hid_rows(k, s, zo, c, start, 32)
            arrived(half, hs.at[p, n], hr.at[p, n])
            m = 7 if n == 4 else 8
            send(half, half, hs.at[p, m], hr.at[p, m], sibling)

    def project(k, s, j):
        p = 2 * k + s
        zz = (z, zm, zp, zo)[j]
        if j == 0:
            arrived(hid_rows(k, s, z, 1 - c), hs.at[p, 0], hr.at[p, 0])
        elif j == 1:
            arrived(hid_rows(k, s, zm, 1 - c), hs.at[p, 3], hr.at[p, 3])
        elif j == 2:
            arrived(hid_rows(k, s, zp, 1 - c), hs.at[p, 5], hr.at[p, 5])
        else:
            arrived(hid_rows(k, s, zo, 1 - c, 0, 32), hs.at[p, 7], hr.at[p, 7])
            arrived(hid_rows(k, s, zo, 1 - c, 32, 32), hs.at[p, 8], hr.at[p, 8])
        base = pl.multiple_of(128 * zz, 128)
        rows = pl.ds(base, 128)
        there = pl.ds(pl.multiple_of(x_lo * 512 + 128 * zz, 128), 128)
        h = hid[k, s, rows, :]
        low = mm_nt(h, vred_t[...])
        lowvt[k, s, x_lo, :, rows] = low.T.astype(BF16)
        add = mm(low.astype(BF16), lift2[...])
        mixed = mm(h, wall[...])
        q[s, rows, 0:128] = (mixed[:, 0:128] * 0.125).astype(BF16)
        q[s, rows, 128:256] = (mixed[:, 384:512] * 0.125).astype(BF16)
        kv[k, s, there, 0:128] = mixed[:, 128:256].astype(BF16)
        kv[k, s, there, 128:256] = (mixed[:, 256:384] + add[:, 0:128]).astype(BF16)
        kv[k, s, there, 256:384] = mixed[:, 512:640].astype(BF16)
        kv[k, s, there, 384:512] = (mixed[:, 640:768] + add[:, 128:256]).astype(BF16)
        region = kv.at[k, s, there, :]
        send(region, region, ks.at[p, j], kr.at[p, j], partner)
        if j == 3:
            region = lowvt.at[k, s, x_lo]
            send(region, region, ks.at[p, 4], kr.at[p, 4], partner)

    def attention(k, s):
        p = 2 * k + s
        with jax.named_scope("keys_arrive"):
            for j in range(4):
                zz = (z, zm, zp, zo)[j]
                there = pl.ds(pl.multiple_of((1 - x_lo) * 512 + 128 * zz, 128), 128)
                arrived(kv.at[k, s, there, :], ks.at[p, j], kr.at[p, j])
            arrived(lowvt.at[k, s, 1 - x_lo], ks.at[p, 4], kr.at[p, 4])
        lower = lax.broadcasted_iota(jnp.int32, (512, 128), 1) < 64
        for n in range(2):
            lanes = slice(128 * n, 128 * n + 128)
            q2 = q[s, :, lanes].astype(F32)
            do2 = dout[p, :, lanes].astype(F32)
            k2 = kv[k, s, :, 256 * n:256 * n + 128]
            v2 = kv[k, s, :, 256 * n + 128:256 * n + 256]
            outs = []
            total = None
            for h in range(2):
                mask = lower if h == 0 else jnp.logical_not(lower)
                st = mm_nt(k2, jnp.where(mask, q2, 0.0).astype(BF16))
                e = jnp.exp(st - jnp.max(st, axis=0, keepdims=True))
                probs = (e * (1.0 / jnp.sum(e, axis=0, keepdims=True))).astype(BF16)
                outs.append(mm_tn(probs, v2))
                term = mm(probs, jnp.where(mask, do2, 0.0).astype(BF16))
                total = term if total is None else total + term
            dv[:, lanes] = total.astype(BF16)
            att_src[k, s, :, lanes] = jnp.where(lower, outs[0], outs[1]).astype(BF16)
        mine = pl.ds(pl.multiple_of(256 * group, 256), 256)
        for d in range(1, 8):
            g = (group + d) % 8
            send(
                att_src.at[k, s, pl.ds(pl.multiple_of(64 * g, 64), 64), :],
                att.at[k, s, :, mine],
                as_.at[p, d],
                ar.at[p, d],
                {"seq": x_lo * 8 + g, "fsdp": fs},
            )
        att[k, s, :, mine] = att_src[k, s, own_rows, :]

    def values_gradient(k, s):
        dvb = dv[...]
        r2_sum[0:32, :] += mm(lowvt[k, s, 0], dvb[0:512]) + mm(lowvt[k, s, 1], dvb[512:1024])
        dlv[s] = mm_nt(lift2[...], dvb)

    def send_low_values(k):
        lower = lax.broadcasted_iota(jnp.int32, (32, 128), 1) < 64
        for j in range(8):
            b0, b1 = dlv[0, :, 128 * j:128 * j + 128], dlv[1, :, 128 * j:128 * j + 128]
            dl_src[k, 2 * j] = jnp.where(lower, b0, pltpu.roll(b1, 64, 1))
            dl_src[k, 2 * j + 1] = jnp.where(lower, pltpu.roll(b0, 64, 1), b1)
        for d in range(1, 16):
            to = (me + d) % 16
            send(
                dl_src.at[k, to], dl_in.at[k, d], ts.at[k, d], tr.at[k, d], {"seq": to, "fsdp": fs}
            )

    def reducer_gradient(k):
        total = jnp.zeros((32, 256), F32)
        for g in range(8):
            both = jnp.concatenate(
                [att_src[k, 0, 64 * g:64 * g + 64, :], att_src[k, 1, 64 * g:64 * g + 64, :]], axis=0
            )
            total = total + mm(dlo[g, 32 * k:32 * k + 32, :], both)
        r2_sum[32:64, :] += total

    def down_gradient(k):
        total = dl_src[k, me]
        for d in range(1, 16):
            arrived(dl_in.at[k, d], ts.at[k, d], tr.at[k, d])
            total = total + dl_in[k, d]
        both = jnp.concatenate([hid[k, 0, own_rows, :], hid[k, 1, own_rows, :]], axis=0)
        gav[...] += mm(total.astype(BF16), both)

    def outlet(k, s):
        p = 2 * k + s
        with jax.named_scope("heads_arrive"):
            for d in range(1, 8):
                g = (group + 8 - d) % 8
                region = att.at[k, s, :, pl.ds(pl.multiple_of(256 * g, 256), 256)]
                arrived(region, as_.at[p, d], ar.at[p, d])
        keep, push, spread = plan(k)
        a = att[k, s]
        low = mm_nt(a, redp[...])
        lowb = low.astype(BF16)
        rows = slice(128 * k + 64 * s, 128 * k + 64 * s + 64)
        gup[...] += mm(low.T.astype(BF16), dvel[rows, :])
        for start in range(0, WIDTH, 512):
            stop = min(start + 512, WIDTH)
            v = mm(a, ep[:, start:stop]) + mm(lowb, olift[:, start:stop])
            old = x0[s, :, start:stop] if k == 0 else x_out[s, :, start:stop]
            x_out[s, :, start:stop] = keep * old + push * v + spread * draws[k, s, :, start:stop]

    with jax.named_scope("entry"):
        pl.semaphore_wait(barrier, 23)
    half = WIDTH // 2
    for n, step in ((0, 1), (1, 3)):
        region = wall.at[pl.ds(n * half, half), pl.ds(own_w, 384)]
        send(region, region, ws.at[n], wr.at[n], x_neighbour(step))
    x_load.wait()
    with jax.named_scope("norm_0_0"):
        norm(0, 0, x0[0])
    with jax.named_scope("gather_start_0_0"):
        gather_start(0, 0)
    with jax.named_scope("norm_0_1"):
        norm(0, 1, x0[1])
    with jax.named_scope("gather_start_0_1"):
        gather_start(0, 1)
    draws_load.wait()

    lift2[:, 0:128] = vlift[:, pl.ds(pl.multiple_of(128 * group, 128), 128)]
    lift2[:, 128:256] = vlift[:, pl.ds(pl.multiple_of(1024 + 128 * group, 128), 128)]
    for g in range(8):
        for h in range(2):
            redp[:, 256 * g + 128 * h:256 * g + 128 * h + 128] = ored_t[
                :, 128 * (8 * h + g):128 * (8 * h + g) + 128
            ]
    r2_sum[...] = jnp.zeros_like(r2_sum)
    gav[...] = jnp.zeros_like(gav)
    gup[...] = jnp.zeros_like(gup)

    for k in range(2):
        keep, push, spread = plan(k)
        coef = -push / (2.0 * SAMPLES * spread)
        for s in range(2):
            start = 128 * k + 64 * s
            dvel[start:start + 64, :] = ((coef * rewards[s]) * draws[k, s]).astype(BF16)
    with jax.named_scope("low_back"):
        low = mm_nt(dvel[...], olift[...])
        lowb = low.astype(BF16)
        low_t = low.T.astype(BF16)
        for k in range(2):
            dlo_src[32 * k:32 * k + 32, :] = low_t[:, 128 * k:128 * k + 128]

    for d in range(1, 8):
        g = (group + d) % 8
        send(dlo_src, dlo.at[group], ls.at[d], lr.at[d], {"seq": x_lo * 8 + g, "fsdp": fs})
    dlo[group] = dlo_src[...]

    with jax.named_scope("gather_near_0_0"):
        gather_near(0, 0)
    with jax.named_scope("loads"):
        for copy in loads:
            copy.wait()

    def outlet_back(g, _):
        rows = pl.ds(pl.multiple_of(256 * g, 256), 256)
        d = mm_nt(dvel[...], ep[rows, :]) + mm(lowb, redp[:, rows])
        dsend[g] = d.astype(BF16).reshape(4, 64, 256)
        return 0

    with jax.named_scope("outlet_back"):
        lax.fori_loop(0, 8, outlet_back, 0)
    with jax.named_scope("gather_near_0_1"):
        gather_near(0, 1)
    with jax.named_scope("gather_far_0_0"):
        gather_far(0, 0)
    for d in range(1, 8):
        g = (group + d) % 8
        send(
            dsend.at[g],
            dout.at[:, own_rows, :],
            ds_.at[d],
            dr.at[d],
            {"seq": x_lo * 8 + g, "fsdp": fs},
        )
    dout[:, own_rows, :] = dsend[group]
    with jax.named_scope("gather_far_0_1"):
        gather_far(0, 1)
    for n in range(2):
        region = wall.at[pl.ds(n * half, half), pl.ds(pl.multiple_of((1 - x_lo) * 384, 128), 384)]
        with jax.named_scope("projection_arrives"):
            arrived(region, ws.at[n], wr.at[n])

    for s in range(2):
        for j in range(4):
            with jax.named_scope(f"project_0_{s}_{j}"):
                project(0, s, j)
    for d in range(1, 8):
        g = (group + 8 - d) % 8
        rows = pl.ds(pl.multiple_of(64 * g, 64), 64)
        arrived(dout.at[:, rows, :], ds_.at[d], dr.at[d])
        arrived(dlo.at[g], ls.at[d], lr.at[d])

    with jax.named_scope("attention_0_0"):
        attention(0, 0)
    with jax.named_scope("values_gradient_0_0"):
        values_gradient(0, 0)
    with jax.named_scope("outlet_0_0"):
        outlet(0, 0)
    with jax.named_scope("norm_1_0"):
        norm(1, 0, x_out[0])
    with jax.named_scope("gather_start_1_0"):
        gather_start(1, 0)
    with jax.named_scope("attention_0_1"):
        attention(0, 1)
    with jax.named_scope("gather_near_1_0"):
        gather_near(1, 0)
    with jax.named_scope("values_gradient_0_1"):
        values_gradient(0, 1)
    with jax.named_scope("send_low_values_0"):
        send_low_values(0)
    with jax.named_scope("gather_far_1_0"):
        gather_far(1, 0)
    for j in range(4):
        with jax.named_scope(f"project_1_0_{j}"):
            project(1, 0, j)
    with jax.named_scope("outlet_0_1"):
        outlet(0, 1)
    with jax.named_scope("norm_1_1"):
        norm(1, 1, x_out[1])
    with jax.named_scope("gather_start_1_1"):
        gather_start(1, 1)
    with jax.named_scope("reducer_gradient_0"):
        reducer_gradient(0)
    with jax.named_scope("down_gradient_0"):
        down_gradient(0)
    with jax.named_scope("gather_near_1_1"):
        gather_near(1, 1)
    with jax.named_scope("attention_1_0"):
        attention(1, 0)
    with jax.named_scope("gather_far_1_1"):
        gather_far(1, 1)
    for j in range(4):
        with jax.named_scope(f"project_1_1_{j}"):
            project(1, 1, j)
    with jax.named_scope("values_gradient_1_0"):
        values_gradient(1, 0)
    with jax.named_scope("outlet_1_0"):
        outlet(1, 0)
    with jax.named_scope("attention_1_1"):
        attention(1, 1)
    with jax.named_scope("values_gradient_1_1"):
        values_gradient(1, 1)
    with jax.named_scope("send_low_values_1"):
        send_low_values(1)
    with jax.named_scope("reducer_gradient_1"):
        reducer_gradient(1)
    send(
        r2_sum.at[:, pl.ds(pl.multiple_of((1 - x_lo) * 128, 128), 128)], r_in, s2, t2, partner
    )
    with jax.named_scope("outlet_1_1"):
        outlet(1, 1)
    with jax.named_scope("down_gradient_1"):
        down_gradient(1)

    part = WIDTH // 16
    with jax.named_scope("wide_parts"):
        for t in range(16):
            a_src[t] = jnp.concatenate(
                [
                    gav[:, part * t:part * t + part],
                    gup[:, part * t:part * t + part],
                    jnp.zeros((RANK, 384 - 2 * part), F32),
                ],
                axis=1,
            ).astype(BF16)

    for d in range(1, 16):
        to = (me + d) % 16
        send(a_src.at[to], a_in.at[d], s1.at[d], t1.at[d], {"seq": to, "fsdp": fs})
    with jax.named_scope("sums_over_seq"):
        arrived(r_in, s2, t2)
    narrow = r2_sum[:, pl.ds(pl.multiple_of(x_lo * 128, 128), 128)] + r_in[...]
    with jax.named_scope("wide_sums"):
        total = a_src[me].astype(F32)
        for d in range(1, 16):
            arrived(a_in.at[d], s1.at[d], t1.at[d])
            total = total + a_in[d].astype(F32)

    step = part // 8
    with jax.named_scope("last_parts"):
        for f in range(8):
            b_src[f] = jnp.concatenate(
                [
                    total[:, step * f:step * f + step],
                    total[:, part + step * f:part + step * f + step],
                    narrow[0:32, 16 * f:16 * f + 16],
                    narrow[32:64, 16 * f:16 * f + 16],
                    jnp.zeros((RANK, 128 - 2 * step - 32), F32),
                ],
                axis=1,
            )

    for d in range(1, 8):
        to = (fs + d) % 8
        send(b_src.at[to], b_in.at[d], s3.at[d], t3.at[d], {"seq": me, "fsdp": to})
    with jax.named_scope("last_sums"):
        total = b_src[fs]
        for d in range(1, 8):
            arrived(b_in.at[d], s3.at[d], t3.at[d])
            total = total + b_in[d]

    sums_out[...] = total.T
    for copy in pending:
        copy.wait_send()


def place_kernel(sums, gav, gup, gbv, gred):
    wide, narrow = gav.shape[0], gbv.shape[0]
    gav[...] = sums[0:wide, :]
    gup[...] = sums[wide:2 * wide, :]
    gbv[...] = sums[2 * wide:2 * wide + narrow, :]
    gred[...] = sums[2 * wide + narrow:2 * wide + 2 * narrow, :]


def per_device(
    perturbed_codes,
    random_draws,
    relative_rewards,
    rescaling_gains,
    triple_projector,
    emission_projector,
    payload_bypass_reducer,
    payload_bypass_lift,
    outlet_bypass_reducer,
    outlet_bypass_lift,
):
    vmem = pl.BlockSpec(memory_space=pltpu.VMEM)
    hbm = pl.BlockSpec(memory_space=pl.ANY)
    dma = pltpu.SemaphoreType.DMA
    final, sums = pl.pallas_call(
        block_kernel,
        out_shape=(
            jax.ShapeDtypeStruct((2, 64, WIDTH), F32),
            jax.ShapeDtypeStruct((128, RANK), F32),
        ),
        in_specs=[
            hbm, hbm, pl.BlockSpec(memory_space=pltpu.SMEM), vmem, hbm,
            hbm, vmem, vmem, vmem, vmem,
        ],
        out_specs=(vmem, vmem),
        scratch_shapes=[
            pltpu.VMEM((2, 64, WIDTH), F32),
            pltpu.VMEM((2, 2, 64, WIDTH), F32),
            pltpu.VMEM((WIDTH, 384), BF16),
            pltpu.VMEM((64, 256), F32),
            pltpu.VMEM((16, RANK, 384), BF16),
            pltpu.VMEM((16, RANK, 384), BF16),
            pltpu.VMEM((64, 128), F32),
            pltpu.VMEM((8, RANK, 128), F32),
            pltpu.VMEM((8, RANK, 128), F32),
            pltpu.VMEM((WIDTH, 768), BF16),
            pltpu.VMEM((INNER, WIDTH), BF16),
            pltpu.VMEM((2, 2, 512, WIDTH), BF16),
            pltpu.VMEM((2, 512, 256), BF16),
            pltpu.VMEM((2, 2, 1024, 512), BF16),
            pltpu.VMEM((2, 2, 2, RANK, 512), BF16),
            pltpu.VMEM((4, 512, 256), BF16),
            pltpu.VMEM((8, 4, 64, 256), BF16),
            pltpu.VMEM((8, 64, 128), BF16),
            pltpu.VMEM((64, 128), BF16),
            pltpu.VMEM((RANK, INNER), BF16),
            pltpu.VMEM((RANK, 256), BF16),
            pltpu.VMEM((2, 2, 64, INNER), BF16),
            pltpu.VMEM((2, 2, 512, 256), BF16),
            pltpu.VMEM((256, WIDTH), BF16),
            pltpu.VMEM((1024, 256), BF16),
            pltpu.VMEM((2, RANK, 1024), F32),
            pltpu.VMEM((2, 16, RANK, 128), F32),
            pltpu.VMEM((2, 16, RANK, 128), F32),
            pltpu.VMEM((RANK, WIDTH), F32),
            pltpu.VMEM((RANK, WIDTH), F32),
            dma((4, 9)), dma((4, 9)),
            dma((4, 5)), dma((4, 5)),
            dma((8,)), dma((8,)),
            dma((8,)), dma((8,)),
            dma((4, 8)), dma((4, 8)),
            dma((2, 16)), dma((2, 16)),
            dma((2,)), dma((2,)),
            dma((16,)),
            dma((16,)), dma((16,)),
            dma, dma,
            dma((8,)), dma((8,)),
            dma((3,)),
        ],
        compiler_params=pltpu.CompilerParams(
            collective_id=0, has_side_effects=True, vmem_limit_bytes=58 * 1024 * 1024
        ),
        name="rollout",
    )(
        perturbed_codes,
        random_draws,
        relative_rewards,
        rescaling_gains.reshape(1, WIDTH),
        triple_projector,
        emission_projector,
        payload_bypass_reducer.T,
        payload_bypass_lift,
        outlet_bypass_reducer.T,
        outlet_bypass_lift,
    )
    wide, narrow = WIDTH // 128, INNER // 128
    gav, gup, gbv, gred = pl.pallas_call(
        place_kernel,
        out_shape=(
            jax.ShapeDtypeStruct((wide, RANK), F32),
            jax.ShapeDtypeStruct((wide, RANK), F32),
            jax.ShapeDtypeStruct((narrow, RANK), F32),
            jax.ShapeDtypeStruct((narrow, RANK), F32),
        ),
        in_specs=[vmem],
        out_specs=(vmem,) * 4,
        name="place",
    )(sums)
    return (final, gav, gbv.T, gred, gup.T)


def solution(mesh):
    placed = (
        P("fsdp", "seq", None),
        P(None, "fsdp", "seq", None),
        P("fsdp"),
        P(),
        P(None, "seq"),
        P(),
        P(),
        P(),
        P(),
        P(),
    )
    return jax.shard_map(
        per_device,
        mesh=mesh,
        in_specs=placed,
        out_specs=(
            P("fsdp", "seq", None),
            P(("seq", "fsdp"), None),
            P(None, ("seq", "fsdp")),
            P(("seq", "fsdp"), None),
            P(None, ("seq", "fsdp")),
        ),
        check_vma=False,
    )
```

```python
import math

import jax
import jax.numpy as jnp
from jax import lax
from jax.experimental import pallas as pl
from jax.experimental.pallas import tpu as pltpu
from jax.sharding import PartitionSpec as P

TIMES = (0.8, 0.7)
STEP = -0.1
LEVEL = 0.7
EPS = 1e-06
SAMPLES = 16
WIDTH = 2432
INNER = 2048
RANK = 32
F32 = jnp.float32
BF16 = jnp.bfloat16
MESH = pl.DeviceIdType.MESH
NT = (((1,), (1,)), ((), ()))
TN = (((0,), (0,)), ((), ()))


def plan(index):
    moment = TIMES[index]
    sigma = LEVEL * math.sqrt(moment / (1.0 - moment))
    drift = sigma * sigma / (2.0 * moment)
    spread = sigma * math.sqrt(-STEP)
    keep = 1.0 + STEP * drift
    push = STEP * (1.0 + drift * (1.0 - moment))
    return (keep, push, spread)


def mm(a, b):
    return jnp.dot(a, b, preferred_element_type=F32)


def mm_nt(a, b):
    return lax.dot_general(a, b, NT, preferred_element_type=F32)


def mm_tn(a, b):
    return lax.dot_general(a, b, TN, preferred_element_type=F32)


def remote(src, dst, send, recv, device):
    return pltpu.make_async_remote_copy(
        src_ref=src,
        dst_ref=dst,
        send_sem=send,
        recv_sem=recv,
        device_id=device,
        device_id_type=MESH,
    )


def block_kernel(
    x_hbm, draws_hbm, rewards, gains, w_hbm, e_hbm, vred_t, vlift, ored_t, olift,
    x_out, sums_out,
    x0, draws, w_in, r2_sum, a_src, a_in, r_in, b_src, b_in,
    wall, ep, hid, q, kv, lowvt, dout, dsend, dlo, dlo_src, redp, lift2,
    att, att_src, dvel, dv, dlv, dl_src, dl_in, gav, gup,
    hs, hr, ks, kr, ds_, dr, ls, lr, as_, ar, ts, tr, ws, wr, es,
    s1, t1, s2, t2, s3, t3, ins,
):
    me = lax.axis_index("seq")
    fs = lax.axis_index("fsdp")
    x_lo, z, c = me // 8, (me // 2) % 4, me % 2
    y, x_hi = fs // 2, fs % 2
    group = z * 2 + c
    zp, zm, zo = (z + 1) % 4, (z + 3) % 4, (z + 2) % 4
    pending = []

    def col(zz, cc):
        return {"seq": (x_lo * 4 + zz) * 2 + cc, "fsdp": fs}

    def x_neighbour(step):
        xx = (x_hi * 2 + x_lo + step) % 4
        return {"seq": ((xx % 2) * 4 + z) * 2 + c, "fsdp": y * 2 + xx // 2}

    sibling = col(z, 1 - c)
    partner = {"seq": (me + 8) % 16, "fsdp": fs}

    def send(src, dst, s, r, device):
        copy = remote(src, dst, s, r, device)
        copy.start()
        pending.append(copy)

    def arrived(region, s, r):
        remote(region, region, s, r, sibling).wait_recv()

    w_load = pltpu.make_async_copy(w_hbm, w_in, ins.at[0])
    x_load = pltpu.make_async_copy(x_hbm, x0, ins.at[1])
    draws_load = pltpu.make_async_copy(draws_hbm, draws, ins.at[2])
    w_load.start()
    x_load.start()
    draws_load.start()

    loads = []
    for g in range(8):
        for h in range(2):
            copy = pltpu.make_async_copy(
                e_hbm.at[pl.ds(128 * (8 * h + g), 128), :],
                ep.at[pl.ds(256 * g + 128 * h, 128), :],
                es.at[2 * g + h],
            )
            copy.start()
            loads.append(copy)

    barrier = pltpu.get_barrier_semaphore()
    for d in range(1, 16):
        pl.semaphore_signal(
            barrier, inc=1, device_id={"seq": (me + d) % 16, "fsdp": fs}, device_id_type=MESH
        )
    outer = x_neighbour(jnp.where(x_lo == 0, -1, 1) + 4)
    pl.semaphore_signal(barrier, inc=1, device_id=outer, device_id_type=MESH)
    for d in range(1, 8):
        pl.semaphore_signal(
            barrier, inc=1, device_id={"seq": me, "fsdp": (fs + d) % 8}, device_id_type=MESH
        )

    low_half = lax.broadcasted_iota(jnp.int32, (128, 128), 1) < 64

    own_w = pl.multiple_of(x_lo * 384, 128)

    def permute(i, _):
        rows = pl.ds(pl.multiple_of(i * 128, 128), 128)
        t0 = w_in[rows, 0:128].astype(F32)
        t1 = w_in[rows, 128:256].astype(F32)
        t2 = w_in[rows, 256:384].astype(F32)
        keys = pltpu.roll(jnp.where(low_half, t2, t0), 64, 1)
        wall[rows, pl.ds(own_w, 128)] = jnp.where(low_half, t0, t1).astype(BF16)
        wall[rows, pl.ds(own_w + 128, 128)] = keys.astype(BF16)
        wall[rows, pl.ds(own_w + 256, 128)] = jnp.where(low_half, t1, t2).astype(BF16)
        return 0

    w_load.wait()
    lax.fori_loop(0, WIDTH // 128, permute, 0)

    def hid_rows(k, s, zz, cc, start=0, size=64):
        return hid.at[k, s, pl.ds(pl.multiple_of(64 * (2 * zz + cc) + start, 32), size), :]

    own_rows = pl.ds(pl.multiple_of(64 * group, 64), 64)

    def norm(k, s, x):
        power = jnp.mean(x * x, axis=-1, keepdims=True)
        h = (x * lax.rsqrt(power + EPS) * gains[...].astype(F32)).astype(BF16)
        hid[k, s, own_rows, :] = h

    def gather_start(k, s):
        p = 2 * k + s
        own = hid_rows(k, s, z, c)
        send(own, own, hs.at[p, 1], hr.at[p, 1], col(zp, c))
        send(own, own, hs.at[p, 2], hr.at[p, 2], col(zm, c))
        send(own, own, hs.at[p, 0], hr.at[p, 0], sibling)

    def gather_near(k, s):
        p = 2 * k + s
        below, above = hid_rows(k, s, zm, c), hid_rows(k, s, zp, c)
        arrived(below, hs.at[p, 1], hr.at[p, 1])
        half = hid_rows(k, s, zm, c, 0, 32)
        send(half, half, hs.at[p, 4], hr.at[p, 4], col(zp, c))
        send(below, below, hs.at[p, 3], hr.at[p, 3], sibling)
        arrived(above, hs.at[p, 2], hr.at[p, 2])
        half = hid_rows(k, s, zp, c, 32, 32)
        send(half, half, hs.at[p, 6], hr.at[p, 6], col(zm, c))
        send(above, above, hs.at[p, 5], hr.at[p, 5], sibling)

    def gather_far(k, s):
        p = 2 * k + s
        for n, start in ((4, 0), (6, 32)):
            half = hid_rows(k, s, zo, c, start, 32)
            arrived(half, hs.at[p, n], hr.at[p, n])
            m = 7 if n == 4 else 8
            send(half, half, hs.at[p, m], hr.at[p, m], sibling)

    def project(k, s, j):
        p = 2 * k + s
        zz = (z, zm, zp, zo)[j]
        if j == 0:
            arrived(hid_rows(k, s, z, 1 - c), hs.at[p, 0], hr.at[p, 0])
        elif j == 1:
            arrived(hid_rows(k, s, zm, 1 - c), hs.at[p, 3], hr.at[p, 3])
        elif j == 2:
            arrived(hid_rows(k, s, zp, 1 - c), hs.at[p, 5], hr.at[p, 5])
        else:
            arrived(hid_rows(k, s, zo, 1 - c, 0, 32), hs.at[p, 7], hr.at[p, 7])
            arrived(hid_rows(k, s, zo, 1 - c, 32, 32), hs.at[p, 8], hr.at[p, 8])
        base = pl.multiple_of(128 * zz, 128)
        rows = pl.ds(base, 128)
        there = pl.ds(pl.multiple_of(x_lo * 512 + 128 * zz, 128), 128)
        h = hid[k, s, rows, :]
        low = mm_nt(h, vred_t[...])
        lowvt[k, s, x_lo, :, rows] = low.T.astype(BF16)
        add = mm(low.astype(BF16), lift2[...])
        mixed = mm(h, wall[...])
        q[s, rows, 0:128] = (mixed[:, 0:128] * 0.125).astype(BF16)
        q[s, rows, 128:256] = (mixed[:, 384:512] * 0.125).astype(BF16)
        kv[k, s, there, 0:128] = mixed[:, 128:256].astype(BF16)
        kv[k, s, there, 128:256] = (mixed[:, 256:384] + add[:, 0:128]).astype(BF16)
        kv[k, s, there, 256:384] = mixed[:, 512:640].astype(BF16)
        kv[k, s, there, 384:512] = (mixed[:, 640:768] + add[:, 128:256]).astype(BF16)
        region = kv.at[k, s, there, :]
        send(region, region, ks.at[p, j], kr.at[p, j], partner)
        if j == 3:
            region = lowvt.at[k, s, x_lo]
            send(region, region, ks.at[p, 4], kr.at[p, 4], partner)

    def attention(k, s):
        p = 2 * k + s
        with jax.named_scope("keys_arrive"):
            for j in range(4):
                zz = (z, zm, zp, zo)[j]
                there = pl.ds(pl.multiple_of((1 - x_lo) * 512 + 128 * zz, 128), 128)
                arrived(kv.at[k, s, there, :], ks.at[p, j], kr.at[p, j])
            arrived(lowvt.at[k, s, 1 - x_lo], ks.at[p, 4], kr.at[p, 4])
        lower = lax.broadcasted_iota(jnp.int32, (512, 128), 1) < 64
        for n in range(2):
            lanes = slice(128 * n, 128 * n + 128)
            q2 = q[s, :, lanes].astype(F32)
            do2 = dout[p, :, lanes].astype(F32)
            k2 = kv[k, s, :, 256 * n:256 * n + 128]
            v2 = kv[k, s, :, 256 * n + 128:256 * n + 256]
            outs = []
            total = None
            for h in range(2):
                mask = lower if h == 0 else jnp.logical_not(lower)
                st = mm_nt(k2, jnp.where(mask, q2, 0.0).astype(BF16))
                e = jnp.exp(st - jnp.max(st, axis=0, keepdims=True))
                probs = (e * (1.0 / jnp.sum(e, axis=0, keepdims=True))).astype(BF16)
                outs.append(mm_tn(probs, v2))
                term = mm(probs, jnp.where(mask, do2, 0.0).astype(BF16))
                total = term if total is None else total + term
            dv[:, lanes] = total.astype(BF16)
            att_src[k, s, :, lanes] = jnp.where(lower, outs[0], outs[1]).astype(BF16)
            mine = pl.ds(pl.multiple_of(256 * group + 128 * n, 128), 128)
            for d in (4, 3, 5, 2, 6, 1, 7):
                g = (group + d) % 8
                send(
                    att_src.at[k, s, pl.ds(pl.multiple_of(64 * g, 64), 64), lanes],
                    att.at[k, s, :, mine],
                    as_.at[p, 8 * n + d],
                    ar.at[p, 8 * n + d],
                    {"seq": x_lo * 8 + g, "fsdp": fs},
                )
            att[k, s, :, mine] = att_src[k, s, own_rows, lanes]

    def values_gradient(k, s):
        dvb = dv[...]
        r2_sum[0:32, :] += mm(lowvt[k, s, 0], dvb[0:512]) + mm(lowvt[k, s, 1], dvb[512:1024])
        dlv[s] = mm_nt(lift2[...], dvb)

    def send_low_values(k):
        lower = lax.broadcasted_iota(jnp.int32, (32, 128), 1) < 64
        for j in range(8):
            b0, b1 = dlv[0, :, 128 * j:128 * j + 128], dlv[1, :, 128 * j:128 * j + 128]
            dl_src[k, 2 * j] = jnp.where(lower, b0, pltpu.roll(b1, 64, 1))
            dl_src[k, 2 * j + 1] = jnp.where(lower, pltpu.roll(b0, 64, 1), b1)
        for d in range(1, 16):
            to = (me + d) % 16
            send(
                dl_src.at[k, to], dl_in.at[k, d], ts.at[k, d], tr.at[k, d], {"seq": to, "fsdp": fs}
            )

    def reducer_gradient(k):
        total = jnp.zeros((32, 256), F32)
        for g in range(8):
            both = jnp.concatenate(
                [att_src[k, 0, 64 * g:64 * g + 64, :], att_src[k, 1, 64 * g:64 * g + 64, :]], axis=0
            )
            total = total + mm(dlo[g, 32 * k:32 * k + 32, :], both)
        r2_sum[32:64, :] += total

    def down_gradient(k):
        total = dl_src[k, me]
        for d in range(1, 16):
            arrived(dl_in.at[k, d], ts.at[k, d], tr.at[k, d])
            total = total + dl_in[k, d]
        both = jnp.concatenate([hid[k, 0, own_rows, :], hid[k, 1, own_rows, :]], axis=0)
        gav[...] += mm(total.astype(BF16), both)

    def outlet(k, s):
        p = 2 * k + s
        with jax.named_scope("heads_arrive"):
            for n in range(2):
                for d in range(1, 8):
                    g = (group + 8 - d) % 8
                    mine = pl.ds(pl.multiple_of(256 * g + 128 * n, 128), 128)
                    arrived(att.at[k, s, :, mine], as_.at[p, 8 * n + d], ar.at[p, 8 * n + d])
        keep, push, spread = plan(k)
        a = att[k, s]
        low = mm_nt(a, redp[...])
        lowb = low.astype(BF16)
        rows = slice(128 * k + 64 * s, 128 * k + 64 * s + 64)
        gup[...] += mm(low.T.astype(BF16), dvel[rows, :])
        for start in range(0, WIDTH, 512):
            stop = min(start + 512, WIDTH)
            v = mm(a, ep[:, start:stop]) + mm(lowb, olift[:, start:stop])
            old = x0[s, :, start:stop] if k == 0 else x_out[s, :, start:stop]
            x_out[s, :, start:stop] = keep * old + push * v + spread * draws[k, s, :, start:stop]

    with jax.named_scope("entry"):
        pl.semaphore_wait(barrier, 23)
    half = WIDTH // 2
    for n, step in ((0, 1), (1, 3)):
        region = wall.at[pl.ds(n * half, half), pl.ds(own_w, 384)]
        send(region, region, ws.at[n], wr.at[n], x_neighbour(step))
    x_load.wait()
    with jax.named_scope("norm_0_0"):
        norm(0, 0, x0[0])
    with jax.named_scope("gather_start_0_0"):
        gather_start(0, 0)
    with jax.named_scope("norm_0_1"):
        norm(0, 1, x0[1])
    with jax.named_scope("gather_start_0_1"):
        gather_start(0, 1)
    draws_load.wait()

    lift2[:, 0:128] = vlift[:, pl.ds(pl.multiple_of(128 * group, 128), 128)]
    lift2[:, 128:256] = vlift[:, pl.ds(pl.multiple_of(1024 + 128 * group, 128), 128)]
    for g in range(8):
        for h in range(2):
            redp[:, 256 * g + 128 * h:256 * g + 128 * h + 128] = ored_t[
                :, 128 * (8 * h + g):128 * (8 * h + g) + 128
            ]
    r2_sum[...] = jnp.zeros_like(r2_sum)
    gav[...] = jnp.zeros_like(gav)
    gup[...] = jnp.zeros_like(gup)

    for k in range(2):
        keep, push, spread = plan(k)
        coef = -push / (2.0 * SAMPLES * spread)
        for s in range(2):
            start = 128 * k + 64 * s
            dvel[start:start + 64, :] = ((coef * rewards[s]) * draws[k, s]).astype(BF16)
    with jax.named_scope("low_back"):
        low = mm_nt(dvel[...], olift[...])
        lowb = low.astype(BF16)
        low_t = low.T.astype(BF16)
        for k in range(2):
            dlo_src[32 * k:32 * k + 32, :] = low_t[:, 128 * k:128 * k + 128]

    for d in range(1, 8):
        g = (group + d) % 8
        send(dlo_src, dlo.at[group], ls.at[d], lr.at[d], {"seq": x_lo * 8 + g, "fsdp": fs})
    dlo[group] = dlo_src[...]

    with jax.named_scope("gather_near_0_0"):
        gather_near(0, 0)
    for copy in loads:
        copy.wait()

    def outlet_back(g, _):
        rows = pl.ds(pl.multiple_of(256 * g, 256), 256)
        d = mm_nt(dvel[...], ep[rows, :]) + mm(lowb, redp[:, rows])
        dsend[g] = d.astype(BF16).reshape(4, 64, 256)
        return 0

    def send_dout(k):
        steps = slice(2 * k, 2 * k + 2)
        for d in range(1, 8):
            g = (group + d) % 8
            send(
                dsend.at[g, steps],
                dout.at[steps, own_rows, :],
                ds_.at[k, d],
                dr.at[k, d],
                {"seq": x_lo * 8 + g, "fsdp": fs},
            )
        dout[steps, own_rows, :] = dsend[group, steps]

    def dout_arrives(k):
        for d in range(1, 8):
            g = (group + 8 - d) % 8
            rows = pl.ds(pl.multiple_of(64 * g, 64), 64)
            arrived(dout.at[2 * k:2 * k + 2, rows, :], ds_.at[k, d], dr.at[k, d])

    with jax.named_scope("outlet_back_low"):
        lax.fori_loop(0, 4, outlet_back, 0)
    with jax.named_scope("gather_far_0_0"):
        gather_far(0, 0)
    with jax.named_scope("outlet_back_high"):
        lax.fori_loop(4, 8, outlet_back, 0)
    with jax.named_scope("gather_near_0_1"):
        gather_near(0, 1)
    for n in range(2):
        region = wall.at[pl.ds(n * half, half), pl.ds(pl.multiple_of((1 - x_lo) * 384, 128), 384)]
        with jax.named_scope("projection_arrives"):
            arrived(region, ws.at[n], wr.at[n])
    with jax.named_scope("project_0_0_0"):
        project(0, 0, 0)
    with jax.named_scope("project_0_0_1"):
        project(0, 0, 1)
    with jax.named_scope("project_0_0_2"):
        project(0, 0, 2)
    with jax.named_scope("project_0_0_3"):
        project(0, 0, 3)
    with jax.named_scope("gather_far_0_1"):
        gather_far(0, 1)
    with jax.named_scope("send_dout_0"):
        send_dout(0)
    with jax.named_scope("project_0_1_0"):
        project(0, 1, 0)
    with jax.named_scope("project_0_1_1"):
        project(0, 1, 1)
    with jax.named_scope("project_0_1_2"):
        project(0, 1, 2)
    with jax.named_scope("project_0_1_3"):
        project(0, 1, 3)
    with jax.named_scope("send_dout_1"):
        send_dout(1)
    with jax.named_scope("dout_arrives_0"):
        dout_arrives(0)
    for d in range(1, 8):
        arrived(dlo.at[(group + 8 - d) % 8], ls.at[d], lr.at[d])
    with jax.named_scope("attention_0_0"):
        attention(0, 0)
    with jax.named_scope("values_gradient_0_0"):
        values_gradient(0, 0)
    with jax.named_scope("outlet_0_0"):
        outlet(0, 0)
    with jax.named_scope("norm_1_0"):
        norm(1, 0, x_out[0])
    with jax.named_scope("gather_start_1_0"):
        gather_start(1, 0)
    with jax.named_scope("project_1_0_0"):
        project(1, 0, 0)
    with jax.named_scope("attention_0_1"):
        attention(0, 1)
    with jax.named_scope("gather_near_1_0"):
        gather_near(1, 0)
    with jax.named_scope("project_1_0_1"):
        project(1, 0, 1)
    with jax.named_scope("project_1_0_2"):
        project(1, 0, 2)
    with jax.named_scope("values_gradient_0_1"):
        values_gradient(0, 1)
    with jax.named_scope("send_low_values_0"):
        send_low_values(0)
    with jax.named_scope("gather_far_1_0"):
        gather_far(1, 0)
    with jax.named_scope("project_1_0_3"):
        project(1, 0, 3)
    with jax.named_scope("outlet_0_1"):
        outlet(0, 1)
    with jax.named_scope("norm_1_1"):
        norm(1, 1, x_out[1])
    with jax.named_scope("gather_start_1_1"):
        gather_start(1, 1)
    with jax.named_scope("project_1_1_0"):
        project(1, 1, 0)
    with jax.named_scope("reducer_gradient_0"):
        reducer_gradient(0)
    with jax.named_scope("down_gradient_0"):
        down_gradient(0)
    with jax.named_scope("dout_arrives_1"):
        dout_arrives(1)
    with jax.named_scope("attention_1_0"):
        attention(1, 0)
    with jax.named_scope("gather_near_1_1"):
        gather_near(1, 1)
    with jax.named_scope("project_1_1_1"):
        project(1, 1, 1)
    with jax.named_scope("project_1_1_2"):
        project(1, 1, 2)
    with jax.named_scope("values_gradient_1_0"):
        values_gradient(1, 0)
    with jax.named_scope("gather_far_1_1"):
        gather_far(1, 1)
    with jax.named_scope("project_1_1_3"):
        project(1, 1, 3)
    with jax.named_scope("outlet_1_0"):
        outlet(1, 0)
    with jax.named_scope("attention_1_1"):
        attention(1, 1)
    with jax.named_scope("values_gradient_1_1"):
        values_gradient(1, 1)
    with jax.named_scope("send_low_values_1"):
        send_low_values(1)
    with jax.named_scope("reducer_gradient_1"):
        reducer_gradient(1)
    send(
        r2_sum.at[:, pl.ds(pl.multiple_of((1 - x_lo) * 128, 128), 128)], r_in, s2, t2, partner
    )
    with jax.named_scope("outlet_1_1"):
        outlet(1, 1)
    with jax.named_scope("down_gradient_1"):
        down_gradient(1)

    part = WIDTH // 16
    with jax.named_scope("wide_parts"):
        for t in range(16):
            a_src[t] = jnp.concatenate(
                [
                    gav[:, part * t:part * t + part],
                    gup[:, part * t:part * t + part],
                    jnp.zeros((RANK, 384 - 2 * part), F32),
                ],
                axis=1,
            ).astype(BF16)

    for d in range(1, 16):
        to = (me + d) % 16
        send(a_src.at[to], a_in.at[d], s1.at[d], t1.at[d], {"seq": to, "fsdp": fs})
    with jax.named_scope("sums_over_seq"):
        arrived(r_in, s2, t2)
    narrow = r2_sum[:, pl.ds(pl.multiple_of(x_lo * 128, 128), 128)] + r_in[...]
    with jax.named_scope("wide_sums"):
        total = a_src[me].astype(F32)
        for d in range(1, 16):
            arrived(a_in.at[d], s1.at[d], t1.at[d])
            total = total + a_in[d].astype(F32)

    step = part // 8
    with jax.named_scope("last_parts"):
        for f in range(8):
            b_src[f] = jnp.concatenate(
                [
                    total[:, step * f:step * f + step],
                    total[:, part + step * f:part + step * f + step],
                    narrow[0:32, 16 * f:16 * f + 16],
                    narrow[32:64, 16 * f:16 * f + 16],
                    jnp.zeros((RANK, 128 - 2 * step - 32), F32),
                ],
                axis=1,
            )

    for d in range(1, 8):
        to = (fs + d) % 8
        send(b_src.at[to], b_in.at[d], s3.at[d], t3.at[d], {"seq": me, "fsdp": to})
    with jax.named_scope("last_sums"):
        total = b_src[fs]
        for d in range(1, 8):
            arrived(b_in.at[d], s3.at[d], t3.at[d])
            total = total + b_in[d]

    sums_out[...] = total.T
    for copy in pending:
        copy.wait_send()


def per_device(
    perturbed_codes,
    random_draws,
    relative_rewards,
    rescaling_gains,
    triple_projector,
    emission_projector,
    payload_bypass_reducer,
    payload_bypass_lift,
    outlet_bypass_reducer,
    outlet_bypass_lift,
):
    vmem = pl.BlockSpec(memory_space=pltpu.VMEM)
    hbm = pl.BlockSpec(memory_space=pl.ANY)
    dma = pltpu.SemaphoreType.DMA
    final, sums = pl.pallas_call(
        block_kernel,
        out_shape=(
            jax.ShapeDtypeStruct((2, 64, WIDTH), F32),
            jax.ShapeDtypeStruct((128, RANK), F32),
        ),
        in_specs=[
            hbm, hbm, pl.BlockSpec(memory_space=pltpu.SMEM), vmem, hbm,
            hbm, vmem, vmem, vmem, vmem,
        ],
        out_specs=(vmem, vmem),
        scratch_shapes=[
            pltpu.VMEM((2, 64, WIDTH), F32),
            pltpu.VMEM((2, 2, 64, WIDTH), F32),
            pltpu.VMEM((WIDTH, 384), BF16),
            pltpu.VMEM((64, 256), F32),
            pltpu.VMEM((16, RANK, 384), BF16),
            pltpu.VMEM((16, RANK, 384), BF16),
            pltpu.VMEM((64, 128), F32),
            pltpu.VMEM((8, RANK, 128), F32),
            pltpu.VMEM((8, RANK, 128), F32),
            pltpu.VMEM((WIDTH, 768), BF16),
            pltpu.VMEM((INNER, WIDTH), BF16),
            pltpu.VMEM((2, 2, 512, WIDTH), BF16),
            pltpu.VMEM((2, 512, 256), BF16),
            pltpu.VMEM((2, 2, 1024, 512), BF16),
            pltpu.VMEM((2, 2, 2, RANK, 512), BF16),
            pltpu.VMEM((4, 512, 256), BF16),
            pltpu.VMEM((8, 4, 64, 256), BF16),
            pltpu.VMEM((8, 64, 128), BF16),
            pltpu.VMEM((64, 128), BF16),
            pltpu.VMEM((RANK, INNER), BF16),
            pltpu.VMEM((RANK, 256), BF16),
            pltpu.VMEM((2, 2, 64, INNER), BF16),
            pltpu.VMEM((2, 2, 512, 256), BF16),
            pltpu.VMEM((256, WIDTH), BF16),
            pltpu.VMEM((1024, 256), BF16),
            pltpu.VMEM((2, RANK, 1024), F32),
            pltpu.VMEM((2, 16, RANK, 128), F32),
            pltpu.VMEM((2, 16, RANK, 128), F32),
            pltpu.VMEM((RANK, WIDTH), F32),
            pltpu.VMEM((RANK, WIDTH), F32),
            dma((4, 9)), dma((4, 9)),
            dma((4, 5)), dma((4, 5)),
            dma((2, 8)), dma((2, 8)),
            dma((8,)), dma((8,)),
            dma((4, 16)), dma((4, 16)),
            dma((2, 16)), dma((2, 16)),
            dma((2,)), dma((2,)),
            dma((16,)),
            dma((16,)), dma((16,)),
            dma, dma,
            dma((8,)), dma((8,)),
            dma((3,)),
        ],
        compiler_params=pltpu.CompilerParams(
            collective_id=0, has_side_effects=True, vmem_limit_bytes=58 * 1024 * 1024
        ),
        name="rollout",
    )(
        perturbed_codes,
        random_draws,
        relative_rewards,
        rescaling_gains.reshape(1, WIDTH),
        triple_projector,
        emission_projector,
        payload_bypass_reducer.T,
        payload_bypass_lift,
        outlet_bypass_reducer.T,
        outlet_bypass_lift,
    )
    wide, narrow = WIDTH // 128, INNER // 128
    ends = (0, wide, 2 * wide, 2 * wide + narrow, 2 * wide + 2 * narrow)
    gav, gup, gbv, gred = (sums[a:b] for a, b in zip(ends, ends[1:]))
    return (final, gav, gbv.T, gred, gup.T)


def solution(mesh):
    placed = (
        P("fsdp", "seq", None),
        P(None, "fsdp", "seq", None),
        P("fsdp"),
        P(),
        P(None, "seq"),
        P(),
        P(),
        P(),
        P(),
        P(),
    )
    return jax.shard_map(
        per_device,
        mesh=mesh,
        in_specs=placed,
        out_specs=(
            P("fsdp", "seq", None),
            P(("seq", "fsdp"), None),
            P(None, ("seq", "fsdp")),
            P(("seq", "fsdp"), None),
            P(None, ("seq", "fsdp")),
        ),
        check_vma=False,
    )
```

```python
import math

import jax
import jax.numpy as jnp
from jax import lax
from jax.experimental import pallas as pl
from jax.experimental.pallas import tpu as pltpu
from jax.sharding import PartitionSpec as P

TIMES = (0.8, 0.7)
STEP = -0.1
LEVEL = 0.7
EPS = 1e-06
SAMPLES = 16
WIDTH = 2432
INNER = 2048
RANK = 32
F32 = jnp.float32
BF16 = jnp.bfloat16
MESH = pl.DeviceIdType.MESH
NT = (((1,), (1,)), ((), ()))
TN = (((0,), (0,)), ((), ()))


def plan(index):
    moment = TIMES[index]
    sigma = LEVEL * math.sqrt(moment / (1.0 - moment))
    drift = sigma * sigma / (2.0 * moment)
    spread = sigma * math.sqrt(-STEP)
    keep = 1.0 + STEP * drift
    push = STEP * (1.0 + drift * (1.0 - moment))
    return (keep, push, spread)


def mm(a, b):
    return jnp.dot(a, b, preferred_element_type=F32)


def mm_nt(a, b):
    return lax.dot_general(a, b, NT, preferred_element_type=F32)


def mm_tn(a, b):
    return lax.dot_general(a, b, TN, preferred_element_type=F32)


def remote(src, dst, send, recv, device):
    return pltpu.make_async_remote_copy(
        src_ref=src,
        dst_ref=dst,
        send_sem=send,
        recv_sem=recv,
        device_id=device,
        device_id_type=MESH,
    )


def block_kernel(
    x_hbm, draws_hbm, rewards, gains, w_hbm, e_hbm, vred_t, vlift, ored_t, olift,
    x_out, sums_out,
    x0, draws, w_in, r2_sum, a_src, a_in, r_in, b_src, b_in,
    wall, ep, hid, kv, lowvt, dout, dsend, dlo, dlo_src, redp, lift2, lift3,
    att, att_src, dvel, dv, dlv, dl_src, dl_in, gav, gup,
    hs, hr, ks, kr, ds_, dr, ls, lr, as_, ar, ts, tr, ws, wr, es,
    s1, t1, s2, t2, s3, t3, ins,
):
    me = lax.axis_index("seq")
    fs = lax.axis_index("fsdp")
    x_lo, z, c = me // 8, (me // 2) % 4, me % 2
    y, x_hi = fs // 2, fs % 2
    group = z * 2 + c
    zp, zm, zo = (z + 1) % 4, (z + 3) % 4, (z + 2) % 4
    pending = []

    def col(zz, cc):
        return {"seq": (x_lo * 4 + zz) * 2 + cc, "fsdp": fs}

    def x_neighbour(step):
        xx = (x_hi * 2 + x_lo + step) % 4
        return {"seq": ((xx % 2) * 4 + z) * 2 + c, "fsdp": y * 2 + xx // 2}

    sibling = col(z, 1 - c)
    partner = {"seq": (me + 8) % 16, "fsdp": fs}

    def send(src, dst, s, r, device):
        copy = remote(src, dst, s, r, device)
        copy.start()
        pending.append(copy)

    def arrived(region, s, r):
        remote(region, region, s, r, sibling).wait_recv()

    w_load = pltpu.make_async_copy(w_hbm, w_in, ins.at[0])
    x_load = pltpu.make_async_copy(x_hbm, x0, ins.at[1])
    draws_load = pltpu.make_async_copy(draws_hbm, draws, ins.at[2])
    w_load.start()
    x_load.start()
    draws_load.start()

    loads = []
    for g in range(8):
        for h in range(2):
            copy = pltpu.make_async_copy(
                e_hbm.at[pl.ds(128 * (8 * h + g), 128), :],
                ep.at[pl.ds(256 * g + 128 * h, 128), :],
                es.at[2 * g + h],
            )
            copy.start()
            loads.append(copy)

    barrier = pltpu.get_barrier_semaphore()
    for d in range(1, 16):
        pl.semaphore_signal(
            barrier, inc=1, device_id={"seq": (me + d) % 16, "fsdp": fs}, device_id_type=MESH
        )
    outer = x_neighbour(jnp.where(x_lo == 0, -1, 1) + 4)
    pl.semaphore_signal(barrier, inc=1, device_id=outer, device_id_type=MESH)
    for d in range(1, 8):
        pl.semaphore_signal(
            barrier, inc=1, device_id={"seq": me, "fsdp": (fs + d) % 8}, device_id_type=MESH
        )

    low_half = lax.broadcasted_iota(jnp.int32, (128, 128), 1) < 64

    def w_columns(n, x):
        return pl.ds(pl.multiple_of(256 * n + 128 * x, 128), 128)

    def permute(i, _):
        rows = pl.ds(pl.multiple_of(i * 128, 128), 128)
        t0 = w_in[rows, 0:128].astype(F32)
        t1 = w_in[rows, 128:256].astype(F32)
        t2 = w_in[rows, 256:384].astype(F32)
        keys = pltpu.roll(jnp.where(low_half, t2, t0), 64, 1)
        wall[rows, w_columns(0, x_lo)] = (jnp.where(low_half, t0, t1) * 0.125).astype(BF16)
        wall[rows, w_columns(1, x_lo)] = keys.astype(BF16)
        wall[rows, w_columns(2, x_lo)] = jnp.where(low_half, t1, t2).astype(BF16)
        return 0

    w_load.wait()
    lax.fori_loop(0, WIDTH // 128, permute, 0)

    def hid_rows(k, s, zz, cc, start=0, size=64):
        return hid.at[k, s, pl.ds(pl.multiple_of(64 * (2 * zz + cc) + start, 32), size), :]

    own_rows = pl.ds(pl.multiple_of(64 * group, 64), 64)

    def norm(k, s, x):
        power = jnp.mean(x * x, axis=-1, keepdims=True)
        h = (x * lax.rsqrt(power + EPS) * gains[...].astype(F32)).astype(BF16)
        hid[k, s, own_rows, :] = h

    def gather_start(k, s):
        p = 2 * k + s
        own = hid_rows(k, s, z, c)
        send(own, own, hs.at[p, 1], hr.at[p, 1], col(zp, c))
        send(own, own, hs.at[p, 2], hr.at[p, 2], col(zm, c))
        send(own, own, hs.at[p, 0], hr.at[p, 0], sibling)

    def gather_near(k, s):
        p = 2 * k + s
        below, above = hid_rows(k, s, zm, c), hid_rows(k, s, zp, c)
        arrived(below, hs.at[p, 1], hr.at[p, 1])
        half = hid_rows(k, s, zm, c, 0, 32)
        send(half, half, hs.at[p, 4], hr.at[p, 4], col(zp, c))
        send(below, below, hs.at[p, 3], hr.at[p, 3], sibling)
        arrived(above, hs.at[p, 2], hr.at[p, 2])
        half = hid_rows(k, s, zp, c, 32, 32)
        send(half, half, hs.at[p, 6], hr.at[p, 6], col(zm, c))
        send(above, above, hs.at[p, 5], hr.at[p, 5], sibling)

    def gather_far(k, s):
        p = 2 * k + s
        for n, start in ((4, 0), (6, 32)):
            half = hid_rows(k, s, zo, c, start, 32)
            arrived(half, hs.at[p, n], hr.at[p, n])
            m = 7 if n == 4 else 8
            send(half, half, hs.at[p, m], hr.at[p, m], sibling)

    def project(k, s, j):
        p = 2 * k + s
        zz = (z, zm, zp, zo)[j]
        if j == 0:
            arrived(hid_rows(k, s, z, 1 - c), hs.at[p, 0], hr.at[p, 0])
        elif j == 1:
            arrived(hid_rows(k, s, zm, 1 - c), hs.at[p, 3], hr.at[p, 3])
        elif j == 2:
            arrived(hid_rows(k, s, zp, 1 - c), hs.at[p, 5], hr.at[p, 5])
        else:
            arrived(hid_rows(k, s, zo, 1 - c, 0, 32), hs.at[p, 7], hr.at[p, 7])
            arrived(hid_rows(k, s, zo, 1 - c, 32, 32), hs.at[p, 8], hr.at[p, 8])
        base = pl.multiple_of(128 * zz, 128)
        rows = pl.ds(base, 128)
        there = pl.ds(pl.multiple_of(x_lo * 512 + 128 * zz, 128), 128)
        low = mm_nt(hid[k, s, rows, :], vred_t[...])
        lowvt[k, s, x_lo, :, rows] = low.T.astype(BF16)
        lowb = low.astype(BF16)

        def third(i, _):
            lanes = pl.ds(pl.multiple_of(256 * i, 256), 256)
            mixed = mm(hid[k, s, rows, :], wall[:, lanes]) + mm(lowb, lift3[:, lanes])
            kv[k, s, there, lanes] = mixed.astype(BF16)
            return 0

        lax.fori_loop(0, 3, third, 0)
        region = kv.at[k, s, there, 256:768]
        send(region, region, ks.at[p, j], kr.at[p, j], partner)
        if j == 3:
            region = lowvt.at[k, s, x_lo]
            send(region, region, ks.at[p, 4], kr.at[p, 4], partner)

    def attention(k, s):
        p = 2 * k + s
        with jax.named_scope("keys_arrive"):
            for j in range(4):
                zz = (z, zm, zp, zo)[j]
                there = pl.ds(pl.multiple_of((1 - x_lo) * 512 + 128 * zz, 128), 128)
                arrived(kv.at[k, s, there, 256:768], ks.at[p, j], kr.at[p, j])
            arrived(lowvt.at[k, s, 1 - x_lo], ks.at[p, 4], kr.at[p, 4])
        lower = lax.broadcasted_iota(jnp.int32, (512, 128), 1) < 64
        queries = pl.ds(pl.multiple_of(x_lo * 512, 512), 512)
        for n in range(2):
            lanes = slice(128 * n, 128 * n + 128)
            q2 = kv[k, s, queries, lanes].astype(F32)
            do2 = dout[p, :, lanes].astype(F32)
            k2 = kv[k, s, :, 256 + 128 * n:384 + 128 * n]
            v2 = kv[k, s, :, 512 + 128 * n:640 + 128 * n]
            outs = []
            total = None
            for h in range(2):
                mask = lower if h == 0 else jnp.logical_not(lower)
                st = mm_nt(k2, jnp.where(mask, q2, 0.0).astype(BF16))
                e = jnp.exp(st - jnp.max(st, axis=0, keepdims=True))
                probs = (e * (1.0 / jnp.sum(e, axis=0, keepdims=True))).astype(BF16)
                outs.append(mm_tn(probs, v2))
                term = mm(probs, jnp.where(mask, do2, 0.0).astype(BF16))
                total = term if total is None else total + term
            dv[:, lanes] = total.astype(BF16)
            att_src[k, s, :, lanes] = jnp.where(lower, outs[0], outs[1]).astype(BF16)
            mine = pl.ds(pl.multiple_of(256 * group + 128 * n, 128), 128)
            for d in (4, 3, 5, 2, 6, 1, 7):
                g = (group + d) % 8
                send(
                    att_src.at[k, s, pl.ds(pl.multiple_of(64 * g, 64), 64), lanes],
                    att.at[k, s, :, mine],
                    as_.at[p, 8 * n + d],
                    ar.at[p, 8 * n + d],
                    {"seq": x_lo * 8 + g, "fsdp": fs},
                )
            att[k, s, :, mine] = att_src[k, s, own_rows, lanes]

    def values_gradient(k, s):
        dvb = dv[...]
        r2_sum[0:32, :] += mm(lowvt[k, s, 0], dvb[0:512]) + mm(lowvt[k, s, 1], dvb[512:1024])
        dlv[s] = mm_nt(lift2[...], dvb)

    def send_low_values(k):
        lower = lax.broadcasted_iota(jnp.int32, (32, 128), 1) < 64
        for j in range(8):
            b0, b1 = dlv[0, :, 128 * j:128 * j + 128], dlv[1, :, 128 * j:128 * j + 128]
            dl_src[k, 2 * j] = jnp.where(lower, b0, pltpu.roll(b1, 64, 1))
            dl_src[k, 2 * j + 1] = jnp.where(lower, pltpu.roll(b0, 64, 1), b1)
        for d in range(1, 16):
            to = (me + d) % 16
            send(
                dl_src.at[k, to], dl_in.at[k, d], ts.at[k, d], tr.at[k, d], {"seq": to, "fsdp": fs}
            )

    def reducer_gradient(k):
        total = jnp.zeros((32, 256), F32)
        for g in range(8):
            both = jnp.concatenate(
                [att_src[k, 0, 64 * g:64 * g + 64, :], att_src[k, 1, 64 * g:64 * g + 64, :]], axis=0
            )
            total = total + mm(dlo[g, 32 * k:32 * k + 32, :], both)
        r2_sum[32:64, :] += total

    def down_gradient(k):
        total = dl_src[k, me]
        for d in range(1, 16):
            arrived(dl_in.at[k, d], ts.at[k, d], tr.at[k, d])
            total = total + dl_in[k, d]
        both = jnp.concatenate([hid[k, 0, own_rows, :], hid[k, 1, own_rows, :]], axis=0)
        gav[...] += mm(total.astype(BF16), both)

    def outlet(k, s):
        p = 2 * k + s
        with jax.named_scope("heads_arrive"):
            for n in range(2):
                for d in range(1, 8):
                    g = (group + 8 - d) % 8
                    mine = pl.ds(pl.multiple_of(256 * g + 128 * n, 128), 128)
                    arrived(att.at[k, s, :, mine], as_.at[p, 8 * n + d], ar.at[p, 8 * n + d])
        keep, push, spread = plan(k)
        a = att[k, s]
        low = mm_nt(a, redp[...])
        lowb = low.astype(BF16)
        rows = slice(128 * k + 64 * s, 128 * k + 64 * s + 64)
        gup[...] += mm(low.T.astype(BF16), dvel[rows, :])
        def update(cols):
            v = mm(att[k, s], ep[:, cols]) + mm(lowb, olift[:, cols])
            old = x0[s, :, cols] if k == 0 else x_out[s, :, cols]
            x_out[s, :, cols] = keep * old + push * v + spread * draws[k, s, :, cols]

        def block(i, _):
            update(pl.ds(pl.multiple_of(512 * i, 512), 512))
            return 0

        lax.fori_loop(0, WIDTH // 512, block, 0)
        update(slice(WIDTH // 512 * 512, WIDTH))

    with jax.named_scope("entry"):
        pl.semaphore_wait(barrier, 23)
    half = WIDTH // 2
    for m in range(3):
        for n, step in ((0, 1), (1, 3)):
            region = wall.at[pl.ds(n * half, half), w_columns(m, x_lo)]
            send(region, region, ws.at[n, m], wr.at[n, m], x_neighbour(step))
    x_load.wait()
    with jax.named_scope("norm_0_0"):
        norm(0, 0, x0[0])
    with jax.named_scope("gather_start_0_0"):
        gather_start(0, 0)
    with jax.named_scope("norm_0_1"):
        norm(0, 1, x0[1])
    with jax.named_scope("gather_start_0_1"):
        gather_start(0, 1)
    draws_load.wait()

    lift2[:, 0:128] = vlift[:, pl.ds(pl.multiple_of(128 * group, 128), 128)]
    lift2[:, 128:256] = vlift[:, pl.ds(pl.multiple_of(1024 + 128 * group, 128), 128)]
    lift3[:, 0:512] = jnp.zeros((RANK, 512), BF16)
    lift3[:, 512:768] = lift2[...]
    for g in range(8):
        for h in range(2):
            redp[:, 256 * g + 128 * h:256 * g + 128 * h + 128] = ored_t[
                :, 128 * (8 * h + g):128 * (8 * h + g) + 128
            ]
    r2_sum[...] = jnp.zeros_like(r2_sum)
    gav[...] = jnp.zeros_like(gav)
    gup[...] = jnp.zeros_like(gup)

    for k in range(2):
        keep, push, spread = plan(k)
        coef = -push / (2.0 * SAMPLES * spread)
        for s in range(2):
            start = 128 * k + 64 * s
            dvel[start:start + 64, :] = ((coef * rewards[s]) * draws[k, s]).astype(BF16)
    with jax.named_scope("low_back"):
        low = mm_nt(dvel[...], olift[...])
        lowb = low.astype(BF16)
        low_t = low.T.astype(BF16)
        for k in range(2):
            dlo_src[32 * k:32 * k + 32, :] = low_t[:, 128 * k:128 * k + 128]

    for d in range(1, 8):
        g = (group + d) % 8
        send(dlo_src, dlo.at[group], ls.at[d], lr.at[d], {"seq": x_lo * 8 + g, "fsdp": fs})
    dlo[group] = dlo_src[...]

    with jax.named_scope("gather_near_0_0"):
        gather_near(0, 0)
    for copy in loads:
        copy.wait()

    def outlet_back(g, _):
        rows = pl.ds(pl.multiple_of(256 * g, 256), 256)
        d = mm_nt(dvel[...], ep[rows, :]) + mm(lowb, redp[:, rows])
        dsend[g] = d.astype(BF16).reshape(4, 64, 256)
        return 0

    def send_dout(k):
        steps = slice(2 * k, 2 * k + 2)
        for d in range(1, 8):
            g = (group + d) % 8
            send(
                dsend.at[g, steps],
                dout.at[steps, own_rows, :],
                ds_.at[k, d],
                dr.at[k, d],
                {"seq": x_lo * 8 + g, "fsdp": fs},
            )
        dout[steps, own_rows, :] = dsend[group, steps]

    def dout_arrives(k):
        for d in range(1, 8):
            g = (group + 8 - d) % 8
            rows = pl.ds(pl.multiple_of(64 * g, 64), 64)
            arrived(dout.at[2 * k:2 * k + 2, rows, :], ds_.at[k, d], dr.at[k, d])

    with jax.named_scope("outlet_back_low"):
        lax.fori_loop(0, 4, outlet_back, 0)
    with jax.named_scope("gather_far_0_0"):
        gather_far(0, 0)
    with jax.named_scope("outlet_back_high"):
        lax.fori_loop(4, 8, outlet_back, 0)
    with jax.named_scope("gather_near_0_1"):
        gather_near(0, 1)
    with jax.named_scope("projection_arrives"):
        for m in range(3):
            for n in range(2):
                region = wall.at[pl.ds(n * half, half), w_columns(m, 1 - x_lo)]
                arrived(region, ws.at[n, m], wr.at[n, m])
    with jax.named_scope("project_0_0_0"):
        project(0, 0, 0)
    with jax.named_scope("project_0_0_1"):
        project(0, 0, 1)
    with jax.named_scope("project_0_0_2"):
        project(0, 0, 2)
    with jax.named_scope("project_0_0_3"):
        project(0, 0, 3)
    with jax.named_scope("gather_far_0_1"):
        gather_far(0, 1)
    with jax.named_scope("send_dout_0"):
        send_dout(0)
    with jax.named_scope("project_0_1_0"):
        project(0, 1, 0)
    with jax.named_scope("project_0_1_1"):
        project(0, 1, 1)
    with jax.named_scope("project_0_1_2"):
        project(0, 1, 2)
    with jax.named_scope("project_0_1_3"):
        project(0, 1, 3)
    with jax.named_scope("send_dout_1"):
        send_dout(1)
    with jax.named_scope("dout_arrives_0"):
        dout_arrives(0)
    for d in range(1, 8):
        arrived(dlo.at[(group + 8 - d) % 8], ls.at[d], lr.at[d])
    with jax.named_scope("attention_0_0"):
        attention(0, 0)
    with jax.named_scope("values_gradient_0_0"):
        values_gradient(0, 0)
    with jax.named_scope("outlet_0_0"):
        outlet(0, 0)
    with jax.named_scope("norm_1_0"):
        norm(1, 0, x_out[0])
    with jax.named_scope("gather_start_1_0"):
        gather_start(1, 0)
    with jax.named_scope("project_1_0_0"):
        project(1, 0, 0)
    with jax.named_scope("attention_0_1"):
        attention(0, 1)
    with jax.named_scope("gather_near_1_0"):
        gather_near(1, 0)
    with jax.named_scope("project_1_0_1"):
        project(1, 0, 1)
    with jax.named_scope("project_1_0_2"):
        project(1, 0, 2)
    with jax.named_scope("values_gradient_0_1"):
        values_gradient(0, 1)
    with jax.named_scope("send_low_values_0"):
        send_low_values(0)
    with jax.named_scope("gather_far_1_0"):
        gather_far(1, 0)
    with jax.named_scope("project_1_0_3"):
        project(1, 0, 3)
    with jax.named_scope("outlet_0_1"):
        outlet(0, 1)
    with jax.named_scope("norm_1_1"):
        norm(1, 1, x_out[1])
    with jax.named_scope("gather_start_1_1"):
        gather_start(1, 1)
    with jax.named_scope("project_1_1_0"):
        project(1, 1, 0)
    with jax.named_scope("reducer_gradient_0"):
        reducer_gradient(0)
    with jax.named_scope("down_gradient_0"):
        down_gradient(0)
    with jax.named_scope("dout_arrives_1"):
        dout_arrives(1)
    with jax.named_scope("attention_1_0"):
        attention(1, 0)
    with jax.named_scope("gather_near_1_1"):
        gather_near(1, 1)
    with jax.named_scope("project_1_1_1"):
        project(1, 1, 1)
    with jax.named_scope("project_1_1_2"):
        project(1, 1, 2)
    with jax.named_scope("values_gradient_1_0"):
        values_gradient(1, 0)
    with jax.named_scope("gather_far_1_1"):
        gather_far(1, 1)
    with jax.named_scope("project_1_1_3"):
        project(1, 1, 3)
    with jax.named_scope("outlet_1_0"):
        outlet(1, 0)
    with jax.named_scope("attention_1_1"):
        attention(1, 1)
    with jax.named_scope("values_gradient_1_1"):
        values_gradient(1, 1)
    with jax.named_scope("send_low_values_1"):
        send_low_values(1)
    with jax.named_scope("reducer_gradient_1"):
        reducer_gradient(1)
    send(
        r2_sum.at[:, pl.ds(pl.multiple_of((1 - x_lo) * 128, 128), 128)], r_in, s2, t2, partner
    )
    with jax.named_scope("outlet_1_1"):
        outlet(1, 1)
    with jax.named_scope("down_gradient_1"):
        down_gradient(1)

    part = WIDTH // 16
    with jax.named_scope("wide_parts"):
        for t in range(16):
            a_src[t] = jnp.concatenate(
                [
                    gav[:, part * t:part * t + part],
                    gup[:, part * t:part * t + part],
                    jnp.zeros((RANK, 384 - 2 * part), F32),
                ],
                axis=1,
            ).astype(BF16)

    for d in range(1, 16):
        to = (me + d) % 16
        send(a_src.at[to], a_in.at[d], s1.at[d], t1.at[d], {"seq": to, "fsdp": fs})
    with jax.named_scope("sums_over_seq"):
        arrived(r_in, s2, t2)
    narrow = r2_sum[:, pl.ds(pl.multiple_of(x_lo * 128, 128), 128)] + r_in[...]
    with jax.named_scope("wide_sums"):
        total = a_src[me].astype(F32)
        for d in range(1, 16):
            arrived(a_in.at[d], s1.at[d], t1.at[d])
            total = total + a_in[d].astype(F32)

    step = part // 8
    with jax.named_scope("last_parts"):
        for f in range(8):
            b_src[f] = jnp.concatenate(
                [
                    total[:, step * f:step * f + step],
                    total[:, part + step * f:part + step * f + step],
                    narrow[0:32, 16 * f:16 * f + 16],
                    narrow[32:64, 16 * f:16 * f + 16],
                    jnp.zeros((RANK, 128 - 2 * step - 32), F32),
                ],
                axis=1,
            )

    for d in range(1, 8):
        to = (fs + d) % 8
        send(b_src.at[to], b_in.at[d], s3.at[d], t3.at[d], {"seq": me, "fsdp": to})
    with jax.named_scope("last_sums"):
        total = b_src[fs]
        for d in range(1, 8):
            arrived(b_in.at[d], s3.at[d], t3.at[d])
            total = total + b_in[d]

    sums_out[...] = total.T
    for copy in pending:
        copy.wait_send()


def per_device(
    perturbed_codes,
    random_draws,
    relative_rewards,
    rescaling_gains,
    triple_projector,
    emission_projector,
    payload_bypass_reducer,
    payload_bypass_lift,
    outlet_bypass_reducer,
    outlet_bypass_lift,
):
    vmem = pl.BlockSpec(memory_space=pltpu.VMEM)
    hbm = pl.BlockSpec(memory_space=pl.ANY)
    dma = pltpu.SemaphoreType.DMA
    final, sums = pl.pallas_call(
        block_kernel,
        out_shape=(
            jax.ShapeDtypeStruct((2, 64, WIDTH), F32),
            jax.ShapeDtypeStruct((128, RANK), F32),
        ),
        in_specs=[
            hbm, hbm, pl.BlockSpec(memory_space=pltpu.SMEM), vmem, hbm,
            hbm, vmem, vmem, vmem, vmem,
        ],
        out_specs=(vmem, vmem),
        scratch_shapes=[
            pltpu.VMEM((2, 64, WIDTH), F32),
            pltpu.VMEM((2, 2, 64, WIDTH), F32),
            pltpu.VMEM((WIDTH, 384), BF16),
            pltpu.VMEM((64, 256), F32),
            pltpu.VMEM((16, RANK, 384), BF16),
            pltpu.VMEM((16, RANK, 384), BF16),
            pltpu.VMEM((64, 128), F32),
            pltpu.VMEM((8, RANK, 128), F32),
            pltpu.VMEM((8, RANK, 128), F32),
            pltpu.VMEM((WIDTH, 768), BF16),
            pltpu.VMEM((INNER, WIDTH), BF16),
            pltpu.VMEM((2, 2, 512, WIDTH), BF16),
            pltpu.VMEM((2, 2, 1024, 768), BF16),
            pltpu.VMEM((2, 2, 2, RANK, 512), BF16),
            pltpu.VMEM((4, 512, 256), BF16),
            pltpu.VMEM((8, 4, 64, 256), BF16),
            pltpu.VMEM((8, 64, 128), BF16),
            pltpu.VMEM((64, 128), BF16),
            pltpu.VMEM((RANK, INNER), BF16),
            pltpu.VMEM((RANK, 256), BF16),
            pltpu.VMEM((RANK, 768), BF16),
            pltpu.VMEM((2, 2, 64, INNER), BF16),
            pltpu.VMEM((2, 2, 512, 256), BF16),
            pltpu.VMEM((256, WIDTH), BF16),
            pltpu.VMEM((1024, 256), BF16),
            pltpu.VMEM((2, RANK, 1024), F32),
            pltpu.VMEM((2, 16, RANK, 128), F32),
            pltpu.VMEM((2, 16, RANK, 128), F32),
            pltpu.VMEM((RANK, WIDTH), F32),
            pltpu.VMEM((RANK, WIDTH), F32),
            dma((4, 9)), dma((4, 9)),
            dma((4, 5)), dma((4, 5)),
            dma((2, 8)), dma((2, 8)),
            dma((8,)), dma((8,)),
            dma((4, 16)), dma((4, 16)),
            dma((2, 16)), dma((2, 16)),
            dma((2, 3)), dma((2, 3)),
            dma((16,)),
            dma((16,)), dma((16,)),
            dma, dma,
            dma((8,)), dma((8,)),
            dma((3,)),
        ],
        compiler_params=pltpu.CompilerParams(
            collective_id=0, has_side_effects=True, vmem_limit_bytes=58 * 1024 * 1024
        ),
        name="rollout",
    )(
        perturbed_codes,
        random_draws,
        relative_rewards,
        rescaling_gains.reshape(1, WIDTH),
        triple_projector,
        emission_projector,
        payload_bypass_reducer.T,
        payload_bypass_lift,
        outlet_bypass_reducer.T,
        outlet_bypass_lift,
    )
    wide, narrow = WIDTH // 128, INNER // 128
    ends = (0, wide, 2 * wide, 2 * wide + narrow, 2 * wide + 2 * narrow)
    gav, gup, gbv, gred = (sums[a:b] for a, b in zip(ends, ends[1:]))
    return (final, gav, gbv.T, gred, gup.T)


def solution(mesh):
    placed = (
        P("fsdp", "seq", None),
        P(None, "fsdp", "seq", None),
        P("fsdp"),
        P(),
        P(None, "seq"),
        P(),
        P(),
        P(),
        P(),
        P(),
    )
    return jax.shard_map(
        per_device,
        mesh=mesh,
        in_specs=placed,
        out_specs=(
            P("fsdp", "seq", None),
            P(("seq", "fsdp"), None),
            P(None, ("seq", "fsdp")),
            P(("seq", "fsdp"), None),
            P(None, ("seq", "fsdp")),
        ),
        check_vma=False,
    )
```

```python
import math

import jax
import jax.numpy as jnp
from jax import lax
from jax.experimental import pallas as pl
from jax.experimental.pallas import tpu as pltpu
from jax.sharding import PartitionSpec as P

TIMES = (0.8, 0.7)
STEP = -0.1
LEVEL = 0.7
EPS = 1e-06
SAMPLES = 16
WIDTH = 2432
INNER = 2048
RANK = 32
F32 = jnp.float32
BF16 = jnp.bfloat16
MESH = pl.DeviceIdType.MESH
NT = (((1,), (1,)), ((), ()))
TN = (((0,), (0,)), ((), ()))


def plan(index):
    moment = TIMES[index]
    sigma = LEVEL * math.sqrt(moment / (1.0 - moment))
    drift = sigma * sigma / (2.0 * moment)
    spread = sigma * math.sqrt(-STEP)
    keep = 1.0 + STEP * drift
    push = STEP * (1.0 + drift * (1.0 - moment))
    return (keep, push, spread)


def mm(a, b):
    return jnp.dot(a, b, preferred_element_type=F32)


def mm_nt(a, b):
    return lax.dot_general(a, b, NT, preferred_element_type=F32)


def mm_tn(a, b):
    return lax.dot_general(a, b, TN, preferred_element_type=F32)


def remote(src, dst, send, recv, device):
    return pltpu.make_async_remote_copy(
        src_ref=src,
        dst_ref=dst,
        send_sem=send,
        recv_sem=recv,
        device_id=device,
        device_id_type=MESH,
    )


def block_kernel(
    x_hbm, draws_hbm, rewards, gains, w_hbm, e_hbm, vred_t, vlift, ored_t, olift,
    x_out, sums_out,
    x0, draws, w_in, r2_sum, a_src, a_in, r_in, b_src, b_in,
    wall, ep, hid, kv, lowvt, dout, dsend, dlo, dlo_src, redp, lift2, lift3,
    att, att_src, dvel, dv, dlv, dl_src, dl_in, gav, gup,
    hs, hr, ks, kr, ds_, dr, ls, lr, as_, ar, ts, tr, ws, wr, es,
    s1, t1, s2, t2, s3, t3, ins,
):
    me = lax.axis_index("seq")
    fs = lax.axis_index("fsdp")
    x_lo, z, c = me // 8, (me // 2) % 4, me % 2
    y, x_hi = fs // 2, fs % 2
    group = z * 2 + c
    zp, zm, zo = (z + 1) % 4, (z + 3) % 4, (z + 2) % 4
    pending = []

    def col(zz, cc):
        return {"seq": (x_lo * 4 + zz) * 2 + cc, "fsdp": fs}

    def x_neighbour(step):
        xx = (x_hi * 2 + x_lo + step) % 4
        return {"seq": ((xx % 2) * 4 + z) * 2 + c, "fsdp": y * 2 + xx // 2}

    sibling = col(z, 1 - c)
    partner = {"seq": (me + 8) % 16, "fsdp": fs}

    def send(src, dst, s, r, device):
        copy = remote(src, dst, s, r, device)
        copy.start()
        pending.append(copy)

    def arrived(region, s, r):
        remote(region, region, s, r, sibling).wait_recv()

    w_load = pltpu.make_async_copy(w_hbm, w_in, ins.at[0])
    x_load = pltpu.make_async_copy(x_hbm, x0, ins.at[1])
    draws_load = pltpu.make_async_copy(draws_hbm, draws, ins.at[2])
    w_load.start()
    x_load.start()
    draws_load.start()

    loads = []
    for g in range(8):
        for h in range(2):
            copy = pltpu.make_async_copy(
                e_hbm.at[pl.ds(128 * (8 * h + g), 128), :],
                ep.at[pl.ds(256 * g + 128 * h, 128), :],
                es.at[2 * g + h],
            )
            copy.start()
            loads.append(copy)

    barrier = pltpu.get_barrier_semaphore()
    for d in range(1, 16):
        pl.semaphore_signal(
            barrier, inc=1, device_id={"seq": (me + d) % 16, "fsdp": fs}, device_id_type=MESH
        )
    outer = x_neighbour(jnp.where(x_lo == 0, -1, 1) + 4)
    pl.semaphore_signal(barrier, inc=1, device_id=outer, device_id_type=MESH)
    for d in range(1, 8):
        pl.semaphore_signal(
            barrier, inc=1, device_id={"seq": me, "fsdp": (fs + d) % 8}, device_id_type=MESH
        )

    low_half = lax.broadcasted_iota(jnp.int32, (128, 128), 1) < 64

    def w_columns(n, x):
        return pl.ds(pl.multiple_of(256 * n + 128 * x, 128), 128)

    def permute(i, _):
        rows = pl.ds(pl.multiple_of(i * 128, 128), 128)
        t0 = w_in[rows, 0:128].astype(F32)
        t1 = w_in[rows, 128:256].astype(F32)
        t2 = w_in[rows, 256:384].astype(F32)
        keys = pltpu.roll(jnp.where(low_half, t2, t0), 64, 1)
        wall[rows, w_columns(0, x_lo)] = (jnp.where(low_half, t0, t1) * 0.125).astype(BF16)
        wall[rows, w_columns(1, x_lo)] = keys.astype(BF16)
        wall[rows, w_columns(2, x_lo)] = jnp.where(low_half, t1, t2).astype(BF16)
        return 0

    w_load.wait()
    lax.fori_loop(0, WIDTH // 128, permute, 0)

    def hid_rows(k, s, zz, cc, start=0, size=64):
        return hid.at[k, s, pl.ds(pl.multiple_of(64 * (2 * zz + cc) + start, 32), size), :]

    own_rows = pl.ds(pl.multiple_of(64 * group, 64), 64)

    def norm(k, s, x):
        power = jnp.mean(x * x, axis=-1, keepdims=True)
        h = (x * lax.rsqrt(power + EPS) * gains[...].astype(F32)[None, :]).astype(BF16)
        hid[k, s, own_rows, :] = h

    def gather_start(k, s):
        p = 2 * k + s
        own = hid_rows(k, s, z, c)
        send(own, own, hs.at[p, 1], hr.at[p, 1], col(zp, c))
        send(own, own, hs.at[p, 2], hr.at[p, 2], col(zm, c))
        send(own, own, hs.at[p, 0], hr.at[p, 0], sibling)

    def gather_near(k, s):
        p = 2 * k + s
        below, above = hid_rows(k, s, zm, c), hid_rows(k, s, zp, c)
        arrived(below, hs.at[p, 1], hr.at[p, 1])
        half = hid_rows(k, s, zm, c, 0, 32)
        send(half, half, hs.at[p, 4], hr.at[p, 4], col(zp, c))
        send(below, below, hs.at[p, 3], hr.at[p, 3], sibling)
        arrived(above, hs.at[p, 2], hr.at[p, 2])
        half = hid_rows(k, s, zp, c, 32, 32)
        send(half, half, hs.at[p, 6], hr.at[p, 6], col(zm, c))
        send(above, above, hs.at[p, 5], hr.at[p, 5], sibling)

    def gather_far(k, s):
        p = 2 * k + s
        for n, start in ((4, 0), (6, 32)):
            half = hid_rows(k, s, zo, c, start, 32)
            arrived(half, hs.at[p, n], hr.at[p, n])
            m = 7 if n == 4 else 8
            send(half, half, hs.at[p, m], hr.at[p, m], sibling)

    def project(k, s, j):
        p = 2 * k + s
        zz = (z, zm, zp, zo)[j]
        if j == 0:
            arrived(hid_rows(k, s, z, 1 - c), hs.at[p, 0], hr.at[p, 0])
        elif j == 1:
            arrived(hid_rows(k, s, zm, 1 - c), hs.at[p, 3], hr.at[p, 3])
        elif j == 2:
            arrived(hid_rows(k, s, zp, 1 - c), hs.at[p, 5], hr.at[p, 5])
        else:
            arrived(hid_rows(k, s, zo, 1 - c, 0, 32), hs.at[p, 7], hr.at[p, 7])
            arrived(hid_rows(k, s, zo, 1 - c, 32, 32), hs.at[p, 8], hr.at[p, 8])
        base = pl.multiple_of(128 * zz, 128)
        rows = pl.ds(base, 128)
        there = pl.ds(pl.multiple_of(x_lo * 512 + 128 * zz, 128), 128)
        low = mm_nt(hid[k, s, rows, :], vred_t[...])
        lowvt[k, s, x_lo, :, rows] = low.T.astype(BF16)
        lowb = low.astype(BF16)

        def third(i, _):
            lanes = pl.ds(pl.multiple_of(256 * i, 256), 256)
            mixed = mm(hid[k, s, rows, :], wall[:, lanes]) + mm(lowb, lift3[:, lanes])
            kv[k, s, there, lanes] = mixed.astype(BF16)
            return 0

        lax.fori_loop(0, 3, third, 0)
        region = kv.at[k, s, there, 256:768]
        send(region, region, ks.at[p, j], kr.at[p, j], partner)
        if j == 3:
            region = lowvt.at[k, s, x_lo]
            send(region, region, ks.at[p, 4], kr.at[p, 4], partner)

    def attention(k, s):
        p = 2 * k + s
        with jax.named_scope("keys_arrive"):
            for j in range(4):
                zz = (z, zm, zp, zo)[j]
                there = pl.ds(pl.multiple_of((1 - x_lo) * 512 + 128 * zz, 128), 128)
                arrived(kv.at[k, s, there, 256:768], ks.at[p, j], kr.at[p, j])
            arrived(lowvt.at[k, s, 1 - x_lo], ks.at[p, 4], kr.at[p, 4])
        lower = lax.broadcasted_iota(jnp.int32, (512, 128), 1) < 64
        queries = pl.ds(pl.multiple_of(x_lo * 512, 512), 512)
        for n in range(2):
            lanes = slice(128 * n, 128 * n + 128)
            q2 = kv[k, s, queries, lanes].astype(F32)
            do2 = dout[p, :, lanes].astype(F32)
            k2 = kv[k, s, :, 256 + 128 * n:384 + 128 * n]
            v2 = kv[k, s, :, 512 + 128 * n:640 + 128 * n]
            outs = []
            total = None
            for h in range(2):
                mask = lower if h == 0 else jnp.logical_not(lower)
                st = mm_nt(k2, jnp.where(mask, q2, 0.0).astype(BF16))
                e = jnp.exp(st - jnp.max(st, axis=0, keepdims=True))
                probs = (e * (1.0 / jnp.sum(e, axis=0, keepdims=True))).astype(BF16)
                outs.append(mm_tn(probs, v2))
                term = mm(probs, jnp.where(mask, do2, 0.0).astype(BF16))
                total = term if total is None else total + term
            dv[:, lanes] = total.astype(BF16)
            att_src[k, s, :, lanes] = jnp.where(lower, outs[0], outs[1]).astype(BF16)
            mine = pl.ds(pl.multiple_of(256 * group + 128 * n, 128), 128)
            for d in (4, 3, 5, 2, 6, 1, 7):
                g = (group + d) % 8
                send(
                    att_src.at[k, s, pl.ds(pl.multiple_of(64 * g, 64), 64), lanes],
                    att.at[k, s, :, mine],
                    as_.at[p, 8 * n + d],
                    ar.at[p, 8 * n + d],
                    {"seq": x_lo * 8 + g, "fsdp": fs},
                )
            att[k, s, :, mine] = att_src[k, s, own_rows, lanes]

    def values_gradient(k, s):
        dvb = dv[...]
        r2_sum[0:32, :] += mm(lowvt[k, s, 0], dvb[0:512]) + mm(lowvt[k, s, 1], dvb[512:1024])
        dlv[s] = mm_nt(lift2[...], dvb)

    def send_low_values(k):
        lower = lax.broadcasted_iota(jnp.int32, (32, 128), 1) < 64
        for j in range(8):
            b0, b1 = dlv[0, :, 128 * j:128 * j + 128], dlv[1, :, 128 * j:128 * j + 128]
            dl_src[k, 2 * j] = jnp.where(lower, b0, pltpu.roll(b1, 64, 1))
            dl_src[k, 2 * j + 1] = jnp.where(lower, pltpu.roll(b0, 64, 1), b1)
        for d in range(1, 16):
            to = (me + d) % 16
            send(
                dl_src.at[k, to], dl_in.at[k, d], ts.at[k, d], tr.at[k, d], {"seq": to, "fsdp": fs}
            )

    def reducer_gradient(k):
        total = jnp.zeros((32, 256), F32)
        for g in range(8):
            both = jnp.concatenate(
                [att_src[k, 0, 64 * g:64 * g + 64, :], att_src[k, 1, 64 * g:64 * g + 64, :]], axis=0
            )
            total = total + mm(dlo[g, 32 * k:32 * k + 32, :], both)
        r2_sum[32:64, :] += total

    def down_gradient(k):
        total = dl_src[k, me]
        for d in range(1, 16):
            arrived(dl_in.at[k, d], ts.at[k, d], tr.at[k, d])
            total = total + dl_in[k, d]
        both = jnp.concatenate([hid[k, 0, own_rows, :], hid[k, 1, own_rows, :]], axis=0)
        gav[...] += mm(total.astype(BF16), both)

    def outlet(k, s):
        p = 2 * k + s
        with jax.named_scope("heads_arrive"):
            for n in range(2):
                for d in range(1, 8):
                    g = (group + 8 - d) % 8
                    mine = pl.ds(pl.multiple_of(256 * g + 128 * n, 128), 128)
                    arrived(att.at[k, s, :, mine], as_.at[p, 8 * n + d], ar.at[p, 8 * n + d])
        keep, push, spread = plan(k)
        a = att[k, s]
        low = mm_nt(a, redp[...])
        lowb = low.astype(BF16)
        rows = slice(128 * k + 64 * s, 128 * k + 64 * s + 64)
        gup[...] += mm(low.T.astype(BF16), dvel[rows, :])
        def update(cols):
            v = mm(att[k, s], ep[:, cols]) + mm(lowb, olift[:, cols])
            old = x0[s, :, cols] if k == 0 else x_out[s, :, cols]
            x_out[s, :, cols] = keep * old + push * v + spread * draws[k, s, :, cols]

        def block(i, _):
            update(pl.ds(pl.multiple_of(512 * i, 512), 512))
            return 0

        lax.fori_loop(0, WIDTH // 512, block, 0)
        update(slice(WIDTH // 512 * 512, WIDTH))

    with jax.named_scope("entry"):
        pl.semaphore_wait(barrier, 23)
    half = WIDTH // 2
    for m in range(3):
        for n, step in ((0, 1), (1, 3)):
            region = wall.at[pl.ds(n * half, half), w_columns(m, x_lo)]
            send(region, region, ws.at[n, m], wr.at[n, m], x_neighbour(step))
    x_load.wait()
    with jax.named_scope("norm_0_0"):
        norm(0, 0, x0[0])
    with jax.named_scope("gather_start_0_0"):
        gather_start(0, 0)
    with jax.named_scope("norm_0_1"):
        norm(0, 1, x0[1])
    with jax.named_scope("gather_start_0_1"):
        gather_start(0, 1)
    draws_load.wait()

    lift2[:, 0:128] = vlift[:, pl.ds(pl.multiple_of(128 * group, 128), 128)]
    lift2[:, 128:256] = vlift[:, pl.ds(pl.multiple_of(1024 + 128 * group, 128), 128)]
    lift3[:, 0:512] = jnp.zeros((RANK, 512), BF16)
    lift3[:, 512:768] = lift2[...]
    for g in range(8):
        for h in range(2):
            redp[:, 256 * g + 128 * h:256 * g + 128 * h + 128] = ored_t[
                :, 128 * (8 * h + g):128 * (8 * h + g) + 128
            ]
    r2_sum[...] = jnp.zeros_like(r2_sum)
    gav[...] = jnp.zeros_like(gav)
    gup[...] = jnp.zeros_like(gup)

    for k in range(2):
        keep, push, spread = plan(k)
        coef = -push / (2.0 * SAMPLES * spread)
        for s in range(2):
            start = 128 * k + 64 * s
            dvel[start:start + 64, :] = ((coef * rewards[s]) * draws[k, s]).astype(BF16)
    with jax.named_scope("low_back"):
        low = mm_nt(dvel[...], olift[...])
        lowb = low.astype(BF16)
        low_t = low.T.astype(BF16)
        for k in range(2):
            dlo_src[32 * k:32 * k + 32, :] = low_t[:, 128 * k:128 * k + 128]

    for d in range(1, 8):
        g = (group + d) % 8
        send(dlo_src, dlo.at[group], ls.at[d], lr.at[d], {"seq": x_lo * 8 + g, "fsdp": fs})
    dlo[group] = dlo_src[...]

    with jax.named_scope("gather_near_0_0"):
        gather_near(0, 0)
    for copy in loads:
        copy.wait()

    def outlet_back(g, _):
        rows = pl.ds(pl.multiple_of(256 * g, 256), 256)
        d = mm_nt(dvel[...], ep[rows, :]) + mm(lowb, redp[:, rows])
        dsend[g] = d.astype(BF16).reshape(4, 64, 256)
        return 0

    def send_dout(k):
        steps = slice(2 * k, 2 * k + 2)
        for d in range(1, 8):
            g = (group + d) % 8
            send(
                dsend.at[g, steps],
                dout.at[steps, own_rows, :],
                ds_.at[k, d],
                dr.at[k, d],
                {"seq": x_lo * 8 + g, "fsdp": fs},
            )
        dout[steps, own_rows, :] = dsend[group, steps]

    def dout_arrives(k):
        for d in range(1, 8):
            g = (group + 8 - d) % 8
            rows = pl.ds(pl.multiple_of(64 * g, 64), 64)
            arrived(dout.at[2 * k:2 * k + 2, rows, :], ds_.at[k, d], dr.at[k, d])

    with jax.named_scope("outlet_back_low"):
        lax.fori_loop(0, 4, outlet_back, 0)
    with jax.named_scope("gather_far_0_0"):
        gather_far(0, 0)
    with jax.named_scope("outlet_back_high"):
        lax.fori_loop(4, 8, outlet_back, 0)
    with jax.named_scope("gather_near_0_1"):
        gather_near(0, 1)
    with jax.named_scope("projection_arrives"):
        for m in range(3):
            for n in range(2):
                region = wall.at[pl.ds(n * half, half), w_columns(m, 1 - x_lo)]
                arrived(region, ws.at[n, m], wr.at[n, m])
    with jax.named_scope("project_0_0_0"):
        project(0, 0, 0)
    with jax.named_scope("project_0_0_1"):
        project(0, 0, 1)
    with jax.named_scope("project_0_0_2"):
        project(0, 0, 2)
    with jax.named_scope("project_0_0_3"):
        project(0, 0, 3)
    with jax.named_scope("gather_far_0_1"):
        gather_far(0, 1)
    with jax.named_scope("send_dout_0"):
        send_dout(0)
    with jax.named_scope("project_0_1_0"):
        project(0, 1, 0)
    with jax.named_scope("project_0_1_1"):
        project(0, 1, 1)
    with jax.named_scope("project_0_1_2"):
        project(0, 1, 2)
    with jax.named_scope("project_0_1_3"):
        project(0, 1, 3)
    with jax.named_scope("send_dout_1"):
        send_dout(1)
    with jax.named_scope("dout_arrives_0"):
        dout_arrives(0)
    for d in range(1, 8):
        arrived(dlo.at[(group + 8 - d) % 8], ls.at[d], lr.at[d])
    with jax.named_scope("attention_0_0"):
        attention(0, 0)
    with jax.named_scope("values_gradient_0_0"):
        values_gradient(0, 0)
    with jax.named_scope("outlet_0_0"):
        outlet(0, 0)
    with jax.named_scope("norm_1_0"):
        norm(1, 0, x_out[0])
    with jax.named_scope("gather_start_1_0"):
        gather_start(1, 0)
    with jax.named_scope("project_1_0_0"):
        project(1, 0, 0)
    with jax.named_scope("attention_0_1"):
        attention(0, 1)
    with jax.named_scope("gather_near_1_0"):
        gather_near(1, 0)
    with jax.named_scope("project_1_0_1"):
        project(1, 0, 1)
    with jax.named_scope("project_1_0_2"):
        project(1, 0, 2)
    with jax.named_scope("values_gradient_0_1"):
        values_gradient(0, 1)
    with jax.named_scope("send_low_values_0"):
        send_low_values(0)
    with jax.named_scope("gather_far_1_0"):
        gather_far(1, 0)
    with jax.named_scope("project_1_0_3"):
        project(1, 0, 3)
    with jax.named_scope("outlet_0_1"):
        outlet(0, 1)
    with jax.named_scope("norm_1_1"):
        norm(1, 1, x_out[1])
    with jax.named_scope("gather_start_1_1"):
        gather_start(1, 1)
    with jax.named_scope("project_1_1_0"):
        project(1, 1, 0)
    with jax.named_scope("reducer_gradient_0"):
        reducer_gradient(0)
    with jax.named_scope("down_gradient_0"):
        down_gradient(0)
    with jax.named_scope("dout_arrives_1"):
        dout_arrives(1)
    with jax.named_scope("attention_1_0"):
        attention(1, 0)
    with jax.named_scope("gather_near_1_1"):
        gather_near(1, 1)
    with jax.named_scope("project_1_1_1"):
        project(1, 1, 1)
    with jax.named_scope("project_1_1_2"):
        project(1, 1, 2)
    with jax.named_scope("values_gradient_1_0"):
        values_gradient(1, 0)
    with jax.named_scope("gather_far_1_1"):
        gather_far(1, 1)
    with jax.named_scope("project_1_1_3"):
        project(1, 1, 3)
    with jax.named_scope("outlet_1_0"):
        outlet(1, 0)
    with jax.named_scope("attention_1_1"):
        attention(1, 1)
    with jax.named_scope("values_gradient_1_1"):
        values_gradient(1, 1)
    with jax.named_scope("send_low_values_1"):
        send_low_values(1)
    with jax.named_scope("reducer_gradient_1"):
        reducer_gradient(1)
    send(
        r2_sum.at[:, pl.ds(pl.multiple_of((1 - x_lo) * 128, 128), 128)], r_in, s2, t2, partner
    )
    with jax.named_scope("outlet_1_1"):
        outlet(1, 1)
    with jax.named_scope("down_gradient_1"):
        down_gradient(1)

    part = WIDTH // 16
    with jax.named_scope("wide_parts"):
        for t in range(16):
            a_src[t] = jnp.concatenate(
                [
                    gav[:, part * t:part * t + part],
                    gup[:, part * t:part * t + part],
                    jnp.zeros((RANK, 384 - 2 * part), F32),
                ],
                axis=1,
            ).astype(BF16)

    for d in range(1, 16):
        to = (me + d) % 16
        send(a_src.at[to], a_in.at[d], s1.at[d], t1.at[d], {"seq": to, "fsdp": fs})
    with jax.named_scope("sums_over_seq"):
        arrived(r_in, s2, t2)
    narrow = r2_sum[:, pl.ds(pl.multiple_of(x_lo * 128, 128), 128)] + r_in[...]
    with jax.named_scope("wide_sums"):
        total = a_src[me].astype(F32)
        for d in range(1, 16):
            arrived(a_in.at[d], s1.at[d], t1.at[d])
            total = total + a_in[d].astype(F32)

    step = part // 8
    with jax.named_scope("last_parts"):
        for f in range(8):
            b_src[f] = jnp.concatenate(
                [
                    total[:, step * f:step * f + step],
                    total[:, part + step * f:part + step * f + step],
                    narrow[0:32, 16 * f:16 * f + 16],
                    narrow[32:64, 16 * f:16 * f + 16],
                    jnp.zeros((RANK, 128 - 2 * step - 32), F32),
                ],
                axis=1,
            )

    for d in range(1, 8):
        to = (fs + d) % 8
        send(b_src.at[to], b_in.at[d], s3.at[d], t3.at[d], {"seq": me, "fsdp": to})
    with jax.named_scope("last_sums"):
        total = b_src[fs]
        for d in range(1, 8):
            arrived(b_in.at[d], s3.at[d], t3.at[d])
            total = total + b_in[d]

    sums_out[...] = total.T
    for copy in pending:
        copy.wait_send()


def per_device(
    perturbed_codes,
    random_draws,
    relative_rewards,
    rescaling_gains,
    triple_projector,
    emission_projector,
    payload_bypass_reducer,
    payload_bypass_lift,
    outlet_bypass_reducer,
    outlet_bypass_lift,
):
    vmem = pl.BlockSpec(memory_space=pltpu.VMEM)
    hbm = pl.BlockSpec(memory_space=pl.ANY)
    dma = pltpu.SemaphoreType.DMA
    final, sums = pl.pallas_call(
        block_kernel,
        out_shape=(
            jax.ShapeDtypeStruct((2, 64, WIDTH), F32),
            jax.ShapeDtypeStruct((128, RANK), F32),
        ),
        in_specs=[
            hbm, hbm, pl.BlockSpec(memory_space=pltpu.SMEM), vmem, hbm,
            hbm, vmem, vmem, vmem, vmem,
        ],
        out_specs=(vmem, vmem),
        scratch_shapes=[
            pltpu.VMEM((2, 64, WIDTH), F32),
            pltpu.VMEM((2, 2, 64, WIDTH), F32),
            pltpu.VMEM((WIDTH, 384), BF16),
            pltpu.VMEM((64, 256), F32),
            pltpu.VMEM((16, RANK, 384), BF16),
            pltpu.VMEM((16, RANK, 384), BF16),
            pltpu.VMEM((64, 128), F32),
            pltpu.VMEM((8, RANK, 128), F32),
            pltpu.VMEM((8, RANK, 128), F32),
            pltpu.VMEM((WIDTH, 768), BF16),
            pltpu.VMEM((INNER, WIDTH), BF16),
            pltpu.VMEM((2, 2, 512, WIDTH), BF16),
            pltpu.VMEM((2, 2, 1024, 768), BF16),
            pltpu.VMEM((2, 2, 2, RANK, 512), BF16),
            pltpu.VMEM((4, 512, 256), BF16),
            pltpu.VMEM((8, 4, 64, 256), BF16),
            pltpu.VMEM((8, 64, 128), BF16),
            pltpu.VMEM((64, 128), BF16),
            pltpu.VMEM((RANK, INNER), BF16),
            pltpu.VMEM((RANK, 256), BF16),
            pltpu.VMEM((RANK, 768), BF16),
            pltpu.VMEM((2, 2, 64, INNER), BF16),
            pltpu.VMEM((2, 2, 512, 256), BF16),
            pltpu.VMEM((256, WIDTH), BF16),
            pltpu.VMEM((1024, 256), BF16),
            pltpu.VMEM((2, RANK, 1024), F32),
            pltpu.VMEM((2, 16, RANK, 128), F32),
            pltpu.VMEM((2, 16, RANK, 128), F32),
            pltpu.VMEM((RANK, WIDTH), F32),
            pltpu.VMEM((RANK, WIDTH), F32),
            dma((4, 9)), dma((4, 9)),
            dma((4, 5)), dma((4, 5)),
            dma((2, 8)), dma((2, 8)),
            dma((8,)), dma((8,)),
            dma((4, 16)), dma((4, 16)),
            dma((2, 16)), dma((2, 16)),
            dma((2, 3)), dma((2, 3)),
            dma((16,)),
            dma((16,)), dma((16,)),
            dma, dma,
            dma((8,)), dma((8,)),
            dma((3,)),
        ],
        compiler_params=pltpu.CompilerParams(
            collective_id=0, has_side_effects=True, vmem_limit_bytes=58 * 1024 * 1024
        ),
        name="rollout",
    )(
        perturbed_codes,
        random_draws,
        relative_rewards,
        rescaling_gains,
        triple_projector,
        emission_projector,
        payload_bypass_reducer.T,
        payload_bypass_lift,
        outlet_bypass_reducer.T,
        outlet_bypass_lift,
    )
    wide, narrow = WIDTH // 128, INNER // 128
    ends = (0, wide, 2 * wide, 2 * wide + narrow, 2 * wide + 2 * narrow)
    gav, gup, gbv, gred = (sums[a:b] for a, b in zip(ends, ends[1:]))
    return (final, gav, gbv.T, gred, gup.T)


def solution(mesh):
    placed = (
        P("fsdp", "seq", None),
        P(None, "fsdp", "seq", None),
        P("fsdp"),
        P(),
        P(None, "seq"),
        P(),
        P(),
        P(),
        P(),
        P(),
    )
    return jax.shard_map(
        per_device,
        mesh=mesh,
        in_specs=placed,
        out_specs=(
            P("fsdp", "seq", None),
            P(("seq", "fsdp"), None),
            P(None, ("seq", "fsdp")),
            P(("seq", "fsdp"), None),
            P(None, ("seq", "fsdp")),
        ),
        check_vma=False,
    )
```

```python
import math

import jax
import jax.numpy as jnp
from jax import lax
from jax.experimental import pallas as pl
from jax.experimental.pallas import tpu as pltpu
from jax.sharding import PartitionSpec as P

TIMES = (0.8, 0.7)
STEP = -0.1
LEVEL = 0.7
EPS = 1e-06
SAMPLES = 16
WIDTH = 2432
INNER = 2048
RANK = 32
F32 = jnp.float32
BF16 = jnp.bfloat16
MESH = pl.DeviceIdType.MESH
NT = (((1,), (1,)), ((), ()))
TN = (((0,), (0,)), ((), ()))


def plan(index):
    moment = TIMES[index]
    sigma = LEVEL * math.sqrt(moment / (1.0 - moment))
    drift = sigma * sigma / (2.0 * moment)
    spread = sigma * math.sqrt(-STEP)
    keep = 1.0 + STEP * drift
    push = STEP * (1.0 + drift * (1.0 - moment))
    return (keep, push, spread)


def mm(a, b):
    return jnp.dot(a, b, preferred_element_type=F32)


def mm_nt(a, b):
    return lax.dot_general(a, b, NT, preferred_element_type=F32)


def mm_tn(a, b):
    return lax.dot_general(a, b, TN, preferred_element_type=F32)


def remote(src, dst, send, recv, device):
    return pltpu.make_async_remote_copy(
        src_ref=src,
        dst_ref=dst,
        send_sem=send,
        recv_sem=recv,
        device_id=device,
        device_id_type=MESH,
    )


def block_kernel(
    x_hbm, draws_hbm, rewards, gains, w_hbm, e_hbm, vred_t, vlift, ored_t, olift,
    x_out, sums_out,
    x0, draws, w_in, r2_sum, a_src, a_in, r_in, b_src, b_in,
    wall, ep, hid, kv, lowvt, dout, dsend, dlo, dlo_src, redp, lift2, lift3,
    att, att_src, dvel, dv, dlv, dl_src, dl_in, gav, gup,
    hs, hr, ks, kr, ds_, dr, ls, lr, as_, ar, ts, tr, ws, wr, es,
    s1, t1, s2, t2, s3, t3, ins,
):
    me = lax.axis_index("seq")
    fs = lax.axis_index("fsdp")
    x_lo, z, c = me // 8, (me // 2) % 4, me % 2
    y, x_hi = fs // 2, fs % 2
    group = z * 2 + c
    zp, zm, zo = (z + 1) % 4, (z + 3) % 4, (z + 2) % 4
    pending = []

    def col(zz, cc):
        return {"seq": (x_lo * 4 + zz) * 2 + cc, "fsdp": fs}

    def x_neighbour(step):
        xx = (x_hi * 2 + x_lo + step) % 4
        return {"seq": ((xx % 2) * 4 + z) * 2 + c, "fsdp": y * 2 + xx // 2}

    sibling = col(z, 1 - c)
    partner = {"seq": (me + 8) % 16, "fsdp": fs}

    def send(src, dst, s, r, device):
        copy = remote(src, dst, s, r, device)
        copy.start()
        pending.append(copy)

    def arrived(region, s, r):
        remote(region, region, s, r, sibling).wait_recv()

    w_load = pltpu.make_async_copy(w_hbm, w_in, ins.at[0])
    x_load = pltpu.make_async_copy(x_hbm, x0, ins.at[1])
    draws_load = pltpu.make_async_copy(draws_hbm, draws, ins.at[2])
    w_load.start()
    x_load.start()
    draws_load.start()

    loads = []
    for g in range(8):
        for h in range(2):
            copy = pltpu.make_async_copy(
                e_hbm.at[pl.ds(128 * (8 * h + g), 128), :],
                ep.at[pl.ds(256 * g + 128 * h, 128), :],
                es.at[2 * g + h],
            )
            copy.start()
            loads.append(copy)

    barrier = pltpu.get_barrier_semaphore()
    for d in range(1, 16):
        pl.semaphore_signal(
            barrier, inc=1, device_id={"seq": (me + d) % 16, "fsdp": fs}, device_id_type=MESH
        )
    outer = x_neighbour(jnp.where(x_lo == 0, -1, 1) + 4)
    pl.semaphore_signal(barrier, inc=1, device_id=outer, device_id_type=MESH)
    for d in range(1, 8):
        pl.semaphore_signal(
            barrier, inc=1, device_id={"seq": me, "fsdp": (fs + d) % 8}, device_id_type=MESH
        )

    low_half = lax.broadcasted_iota(jnp.int32, (128, 128), 1) < 64

    def w_columns(n, x):
        return pl.ds(pl.multiple_of(256 * n + 128 * x, 128), 128)

    def permute(i, _):
        rows = pl.ds(pl.multiple_of(i * 128, 128), 128)
        t0 = w_in[rows, 0:128].astype(F32)
        t1 = w_in[rows, 128:256].astype(F32)
        t2 = w_in[rows, 256:384].astype(F32)
        keys = pltpu.roll(jnp.where(low_half, t2, t0), 64, 1)
        wall[rows, w_columns(0, x_lo)] = (jnp.where(low_half, t0, t1) * 0.125).astype(BF16)
        wall[rows, w_columns(1, x_lo)] = keys.astype(BF16)
        wall[rows, w_columns(2, x_lo)] = jnp.where(low_half, t1, t2).astype(BF16)
        return 0

    w_load.wait()
    lax.fori_loop(0, WIDTH // 128, permute, 0)

    def hid_rows(k, s, zz, cc, start=0, size=64):
        return hid.at[k, s, pl.ds(pl.multiple_of(64 * (2 * zz + cc) + start, 32), size), :]

    own_rows = pl.ds(pl.multiple_of(64 * group, 64), 64)

    def norm(k, s, x):
        power = jnp.mean(x * x, axis=-1, keepdims=True)
        h = (x * lax.rsqrt(power + EPS) * gains[...].astype(F32)[None, :]).astype(BF16)
        hid[k, s, own_rows, :] = h

    def gather_start(k, s):
        p = 2 * k + s
        own = hid_rows(k, s, z, c)
        send(own, own, hs.at[p, 1], hr.at[p, 1], col(zp, c))
        send(own, own, hs.at[p, 2], hr.at[p, 2], col(zm, c))
        send(own, own, hs.at[p, 0], hr.at[p, 0], sibling)

    def gather_near(k, s):
        p = 2 * k + s
        below, above = hid_rows(k, s, zm, c), hid_rows(k, s, zp, c)
        arrived(below, hs.at[p, 1], hr.at[p, 1])
        half = hid_rows(k, s, zm, c, 0, 32)
        send(half, half, hs.at[p, 4], hr.at[p, 4], col(zp, c))
        send(below, below, hs.at[p, 3], hr.at[p, 3], sibling)
        arrived(above, hs.at[p, 2], hr.at[p, 2])
        half = hid_rows(k, s, zp, c, 32, 32)
        send(half, half, hs.at[p, 6], hr.at[p, 6], col(zm, c))
        send(above, above, hs.at[p, 5], hr.at[p, 5], sibling)

    def gather_far(k, s):
        p = 2 * k + s
        for n, start in ((4, 0), (6, 32)):
            half = hid_rows(k, s, zo, c, start, 32)
            arrived(half, hs.at[p, n], hr.at[p, n])
            m = 7 if n == 4 else 8
            send(half, half, hs.at[p, m], hr.at[p, m], sibling)

    def project(k, s, j):
        p = 2 * k + s
        zz = (z, zm, zp, zo)[j]
        if j == 0:
            arrived(hid_rows(k, s, z, 1 - c), hs.at[p, 0], hr.at[p, 0])
        elif j == 1:
            arrived(hid_rows(k, s, zm, 1 - c), hs.at[p, 3], hr.at[p, 3])
        elif j == 2:
            arrived(hid_rows(k, s, zp, 1 - c), hs.at[p, 5], hr.at[p, 5])
        else:
            arrived(hid_rows(k, s, zo, 1 - c, 0, 32), hs.at[p, 7], hr.at[p, 7])
            arrived(hid_rows(k, s, zo, 1 - c, 32, 32), hs.at[p, 8], hr.at[p, 8])
        base = pl.multiple_of(128 * zz, 128)
        rows = pl.ds(base, 128)
        there = pl.ds(pl.multiple_of(x_lo * 512 + 128 * zz, 128), 128)
        low = mm_nt(hid[k, s, rows, :], vred_t[...])
        lowvt[k, s, x_lo, :, rows] = low.T.astype(BF16)
        lowb = low.astype(BF16)

        def third(i, _):
            lanes = pl.ds(pl.multiple_of(256 * i, 256), 256)
            mixed = mm(hid[k, s, rows, :], wall[:, lanes]) + mm(lowb, lift3[:, lanes])
            kv[k, s, there, lanes] = mixed.astype(BF16)
            return 0

        lax.fori_loop(0, 3, third, 0)
        region = kv.at[k, s, there, 256:768]
        send(region, region, ks.at[p, j], kr.at[p, j], partner)
        if j == 3:
            region = lowvt.at[k, s, x_lo]
            send(region, region, ks.at[p, 4], kr.at[p, 4], partner)

    def attention(k, s):
        p = 2 * k + s
        with jax.named_scope("keys_arrive"):
            for j in range(4):
                zz = (z, zm, zp, zo)[j]
                there = pl.ds(pl.multiple_of((1 - x_lo) * 512 + 128 * zz, 128), 128)
                arrived(kv.at[k, s, there, 256:768], ks.at[p, j], kr.at[p, j])
            arrived(lowvt.at[k, s, 1 - x_lo], ks.at[p, 4], kr.at[p, 4])
        lower = lax.broadcasted_iota(jnp.int32, (512, 128), 1) < 64
        queries = pl.ds(pl.multiple_of(x_lo * 512, 512), 512)
        for n in range(2):
            lanes = slice(128 * n, 128 * n + 128)
            q2 = kv[k, s, queries, lanes].astype(F32)
            do2 = dout[p, :, lanes].astype(F32)
            k2 = kv[k, s, :, 256 + 128 * n:384 + 128 * n]
            v2 = kv[k, s, :, 512 + 128 * n:640 + 128 * n]
            outs = []
            total = None
            for h in range(2):
                mask = lower if h == 0 else jnp.logical_not(lower)
                st = mm_nt(k2, jnp.where(mask, q2, 0.0).astype(BF16))
                e = jnp.exp(st - jnp.max(st, axis=0, keepdims=True))
                probs = (e * (1.0 / jnp.sum(e, axis=0, keepdims=True))).astype(BF16)
                outs.append(mm_tn(probs, v2))
                term = mm(probs, jnp.where(mask, do2, 0.0).astype(BF16))
                total = term if total is None else total + term
            dv[:, lanes] = total.astype(BF16)
            att_src[k, s, :, lanes] = jnp.where(lower, outs[0], outs[1]).astype(BF16)
            mine = pl.ds(pl.multiple_of(256 * group + 128 * n, 128), 128)
            for d in (4, 3, 5, 2, 6, 1, 7):
                g = (group + d) % 8
                send(
                    att_src.at[k, s, pl.ds(pl.multiple_of(64 * g, 64), 64), lanes],
                    att.at[k, s, :, mine],
                    as_.at[p, 8 * n + d],
                    ar.at[p, 8 * n + d],
                    {"seq": x_lo * 8 + g, "fsdp": fs},
                )
            att[k, s, :, mine] = att_src[k, s, own_rows, lanes]

    def values_gradient(k, s):
        dvb = dv[...]
        r2_sum[0:32, :] += mm(lowvt[k, s, 0], dvb[0:512]) + mm(lowvt[k, s, 1], dvb[512:1024])
        dlv[s] = mm_nt(lift2[...], dvb)

    def send_low_values(k):
        lower = lax.broadcasted_iota(jnp.int32, (32, 128), 1) < 64
        for j in range(8):
            b0, b1 = dlv[0, :, 128 * j:128 * j + 128], dlv[1, :, 128 * j:128 * j + 128]
            dl_src[k, 2 * j] = jnp.where(lower, b0, pltpu.roll(b1, 64, 1))
            dl_src[k, 2 * j + 1] = jnp.where(lower, pltpu.roll(b0, 64, 1), b1)
        for d in range(1, 16):
            to = (me + d) % 16
            send(
                dl_src.at[k, to], dl_in.at[k, d], ts.at[k, d], tr.at[k, d], {"seq": to, "fsdp": fs}
            )

    def reducer_gradient(k):
        total = jnp.zeros((32, 256), F32)
        for g in range(8):
            both = jnp.concatenate(
                [att_src[k, 0, 64 * g:64 * g + 64, :], att_src[k, 1, 64 * g:64 * g + 64, :]], axis=0
            )
            total = total + mm(dlo[g, 32 * k:32 * k + 32, :], both)
        r2_sum[32:64, :] += total

    def down_gradient(k):
        total = dl_src[k, me]
        for d in range(1, 16):
            arrived(dl_in.at[k, d], ts.at[k, d], tr.at[k, d])
            total = total + dl_in[k, d]
        both = jnp.concatenate([hid[k, 0, own_rows, :], hid[k, 1, own_rows, :]], axis=0)
        gav[...] += mm(total.astype(BF16), both)

    def outlet(k, s):
        p = 2 * k + s
        with jax.named_scope("heads_arrive"):
            for n in range(2):
                for d in range(1, 8):
                    g = (group + 8 - d) % 8
                    mine = pl.ds(pl.multiple_of(256 * g + 128 * n, 128), 128)
                    arrived(att.at[k, s, :, mine], as_.at[p, 8 * n + d], ar.at[p, 8 * n + d])
        keep, push, spread = plan(k)
        a = att[k, s]
        low = mm_nt(a, redp[...])
        lowb = low.astype(BF16)
        rows = slice(128 * k + 64 * s, 128 * k + 64 * s + 64)
        gup[...] += mm(low.T.astype(BF16), dvel[rows, :])
        def update(cols):
            v = mm(att[k, s], ep[:, cols]) + mm(lowb, olift[:, cols])
            old = x0[s, :, cols] if k == 0 else x_out[s, :, cols]
            x_out[s, :, cols] = keep * old + push * v + spread * draws[k, s, :, cols]

        def block(i, _):
            update(pl.ds(pl.multiple_of(512 * i, 512), 512))
            return 0

        lax.fori_loop(0, WIDTH // 512, block, 0)
        update(slice(WIDTH // 512 * 512, WIDTH))

    with jax.named_scope("entry"):
        pl.semaphore_wait(barrier, 23)
    half = WIDTH // 2
    for m in range(3):
        for n, step in ((0, 1), (1, 3)):
            region = wall.at[pl.ds(n * half, half), w_columns(m, x_lo)]
            send(region, region, ws.at[n, m], wr.at[n, m], x_neighbour(step))
    x_load.wait()
    with jax.named_scope("norm_0_0"):
        norm(0, 0, x0[0])
    with jax.named_scope("gather_start_0_0"):
        gather_start(0, 0)
    with jax.named_scope("norm_0_1"):
        norm(0, 1, x0[1])
    with jax.named_scope("gather_start_0_1"):
        gather_start(0, 1)
    draws_load.wait()

    lift2[:, 0:128] = vlift[:, pl.ds(pl.multiple_of(128 * group, 128), 128)]
    lift2[:, 128:256] = vlift[:, pl.ds(pl.multiple_of(1024 + 128 * group, 128), 128)]
    lift3[:, 0:512] = jnp.zeros((RANK, 512), BF16)
    lift3[:, 512:768] = lift2[...]
    for g in range(8):
        for h in range(2):
            redp[:, 256 * g + 128 * h:256 * g + 128 * h + 128] = ored_t[
                :, 128 * (8 * h + g):128 * (8 * h + g) + 128
            ]
    r2_sum[...] = jnp.zeros_like(r2_sum)
    gav[...] = jnp.zeros_like(gav)
    gup[...] = jnp.zeros_like(gup)

    for k in range(2):
        keep, push, spread = plan(k)
        coef = -push / (2.0 * SAMPLES * spread)
        for s in range(2):
            start = 128 * k + 64 * s
            dvel[start:start + 64, :] = ((coef * rewards[s]) * draws[k, s]).astype(BF16)
    with jax.named_scope("low_back"):
        low = mm_nt(dvel[...], olift[...])
        lowb = low.astype(BF16)
        low_t = low.T.astype(BF16)
        for k in range(2):
            dlo_src[32 * k:32 * k + 32, :] = low_t[:, 128 * k:128 * k + 128]

    for d in range(1, 8):
        g = (group + d) % 8
        send(dlo_src, dlo.at[group], ls.at[d], lr.at[d], {"seq": x_lo * 8 + g, "fsdp": fs})
    dlo[group] = dlo_src[...]

    with jax.named_scope("gather_near_0_0"):
        gather_near(0, 0)
    for copy in loads:
        copy.wait()

    def outlet_back(g, _):
        rows = pl.ds(pl.multiple_of(256 * g, 256), 256)
        d = mm_nt(dvel[...], ep[rows, :]) + mm(lowb, redp[:, rows])
        dsend[g] = d.astype(BF16).reshape(4, 64, 256)
        return 0

    def send_dout(k):
        steps = slice(2 * k, 2 * k + 2)
        for d in range(1, 8):
            g = (group + d) % 8
            send(
                dsend.at[g, steps],
                dout.at[steps, own_rows, :],
                ds_.at[k, d],
                dr.at[k, d],
                {"seq": x_lo * 8 + g, "fsdp": fs},
            )
        dout[steps, own_rows, :] = dsend[group, steps]

    def dout_arrives(k):
        for d in range(1, 8):
            g = (group + 8 - d) % 8
            rows = pl.ds(pl.multiple_of(64 * g, 64), 64)
            arrived(dout.at[2 * k:2 * k + 2, rows, :], ds_.at[k, d], dr.at[k, d])

    with jax.named_scope("outlet_back_low"):
        lax.fori_loop(0, 4, outlet_back, 0)
    with jax.named_scope("gather_far_0_0"):
        gather_far(0, 0)
    with jax.named_scope("outlet_back_high"):
        lax.fori_loop(4, 8, outlet_back, 0)
    with jax.named_scope("gather_near_0_1"):
        gather_near(0, 1)
    with jax.named_scope("projection_arrives"):
        for m in range(3):
            for n in range(2):
                region = wall.at[pl.ds(n * half, half), w_columns(m, 1 - x_lo)]
                arrived(region, ws.at[n, m], wr.at[n, m])
    with jax.named_scope("project_0_0_0"):
        project(0, 0, 0)
    with jax.named_scope("project_0_0_1"):
        project(0, 0, 1)
    with jax.named_scope("project_0_0_2"):
        project(0, 0, 2)
    with jax.named_scope("project_0_0_3"):
        project(0, 0, 3)
    with jax.named_scope("gather_far_0_1"):
        gather_far(0, 1)
    with jax.named_scope("send_dout_0"):
        send_dout(0)
    with jax.named_scope("project_0_1_0"):
        project(0, 1, 0)
    with jax.named_scope("project_0_1_1"):
        project(0, 1, 1)
    with jax.named_scope("project_0_1_2"):
        project(0, 1, 2)
    with jax.named_scope("project_0_1_3"):
        project(0, 1, 3)
    with jax.named_scope("send_dout_1"):
        send_dout(1)
    with jax.named_scope("dout_arrives_0"):
        dout_arrives(0)
    for d in range(1, 8):
        arrived(dlo.at[(group + 8 - d) % 8], ls.at[d], lr.at[d])
    with jax.named_scope("attention_0_0"):
        attention(0, 0)
    with jax.named_scope("values_gradient_0_0"):
        values_gradient(0, 0)
    with jax.named_scope("outlet_0_0"):
        outlet(0, 0)
    with jax.named_scope("norm_1_0"):
        norm(1, 0, x_out[0])
    with jax.named_scope("gather_start_1_0"):
        gather_start(1, 0)
    with jax.named_scope("project_1_0_0"):
        project(1, 0, 0)
    with jax.named_scope("attention_0_1"):
        attention(0, 1)
    with jax.named_scope("gather_near_1_0"):
        gather_near(1, 0)
    with jax.named_scope("project_1_0_1"):
        project(1, 0, 1)
    with jax.named_scope("project_1_0_2"):
        project(1, 0, 2)
    with jax.named_scope("values_gradient_0_1"):
        values_gradient(0, 1)
    with jax.named_scope("send_low_values_0"):
        send_low_values(0)
    with jax.named_scope("gather_far_1_0"):
        gather_far(1, 0)
    with jax.named_scope("project_1_0_3"):
        project(1, 0, 3)
    with jax.named_scope("outlet_0_1"):
        outlet(0, 1)
    with jax.named_scope("norm_1_1"):
        norm(1, 1, x_out[1])
    with jax.named_scope("gather_start_1_1"):
        gather_start(1, 1)
    with jax.named_scope("project_1_1_0"):
        project(1, 1, 0)
    with jax.named_scope("reducer_gradient_0"):
        reducer_gradient(0)
    with jax.named_scope("down_gradient_0"):
        down_gradient(0)
    with jax.named_scope("dout_arrives_1"):
        dout_arrives(1)
    with jax.named_scope("attention_1_0"):
        attention(1, 0)
    with jax.named_scope("gather_near_1_1"):
        gather_near(1, 1)
    with jax.named_scope("project_1_1_1"):
        project(1, 1, 1)
    with jax.named_scope("project_1_1_2"):
        project(1, 1, 2)
    with jax.named_scope("values_gradient_1_0"):
        values_gradient(1, 0)
    with jax.named_scope("gather_far_1_1"):
        gather_far(1, 1)
    with jax.named_scope("project_1_1_3"):
        project(1, 1, 3)
    with jax.named_scope("outlet_1_0"):
        outlet(1, 0)
    with jax.named_scope("attention_1_1"):
        attention(1, 1)
    with jax.named_scope("values_gradient_1_1"):
        values_gradient(1, 1)
    with jax.named_scope("send_low_values_1"):
        send_low_values(1)
    with jax.named_scope("reducer_gradient_1"):
        reducer_gradient(1)
    send(
        r2_sum.at[:, pl.ds(pl.multiple_of((1 - x_lo) * 128, 128), 128)], r_in, s2, t2, partner
    )
    with jax.named_scope("outlet_1_1"):
        outlet(1, 1)
    part = WIDTH // 16

    def send_wide(n, grad):
        for t in range(16):
            a_src[n, t] = jnp.concatenate(
                [grad[:, part * t:part * t + part], jnp.zeros((RANK, 256 - part), F32)], axis=1
            ).astype(BF16)
        for d in range(1, 16):
            to = (me + d) % 16
            send(
                a_src.at[n, to],
                a_in.at[n, d],
                s1.at[n, d],
                t1.at[n, d],
                {"seq": to, "fsdp": fs},
            )

    def wide_sum(n):
        total = a_src[n, me].astype(F32)
        for d in range(1, 16):
            arrived(a_in.at[n, d], s1.at[n, d], t1.at[n, d])
            total = total + a_in[n, d].astype(F32)
        return total

    with jax.named_scope("send_wide_up"):
        send_wide(1, gup)
    with jax.named_scope("down_gradient_1"):
        down_gradient(1)
    with jax.named_scope("send_wide_down"):
        send_wide(0, gav)
    with jax.named_scope("sums_over_seq"):
        arrived(r_in, s2, t2)
    narrow = r2_sum[:, pl.ds(pl.multiple_of(x_lo * 128, 128), 128)] + r_in[...]
    with jax.named_scope("wide_sums"):
        up_sum = wide_sum(1)
        down_sum = wide_sum(0)

    step = part // 8
    with jax.named_scope("last_parts"):
        for f in range(8):
            b_src[f] = jnp.concatenate(
                [
                    down_sum[:, step * f:step * f + step],
                    up_sum[:, step * f:step * f + step],
                    narrow[0:32, 16 * f:16 * f + 16],
                    narrow[32:64, 16 * f:16 * f + 16],
                    jnp.zeros((RANK, 128 - 2 * step - 32), F32),
                ],
                axis=1,
            )

    for d in range(1, 8):
        to = (fs + d) % 8
        send(b_src.at[to], b_in.at[d], s3.at[d], t3.at[d], {"seq": me, "fsdp": to})
    with jax.named_scope("last_sums"):
        total = b_src[fs]
        for d in range(1, 8):
            arrived(b_in.at[d], s3.at[d], t3.at[d])
            total = total + b_in[d]

    sums_out[...] = total.T
    for copy in pending:
        copy.wait_send()


def per_device(
    perturbed_codes,
    random_draws,
    relative_rewards,
    rescaling_gains,
    triple_projector,
    emission_projector,
    payload_bypass_reducer,
    payload_bypass_lift,
    outlet_bypass_reducer,
    outlet_bypass_lift,
):
    vmem = pl.BlockSpec(memory_space=pltpu.VMEM)
    hbm = pl.BlockSpec(memory_space=pl.ANY)
    dma = pltpu.SemaphoreType.DMA
    final, sums = pl.pallas_call(
        block_kernel,
        out_shape=(
            jax.ShapeDtypeStruct((2, 64, WIDTH), F32),
            jax.ShapeDtypeStruct((128, RANK), F32),
        ),
        in_specs=[
            hbm, hbm, pl.BlockSpec(memory_space=pltpu.SMEM), vmem, hbm,
            hbm, vmem, vmem, vmem, vmem,
        ],
        out_specs=(vmem, vmem),
        scratch_shapes=[
            pltpu.VMEM((2, 64, WIDTH), F32),
            pltpu.VMEM((2, 2, 64, WIDTH), F32),
            pltpu.VMEM((WIDTH, 384), BF16),
            pltpu.VMEM((64, 256), F32),
            pltpu.VMEM((2, 16, RANK, 256), BF16),
            pltpu.VMEM((2, 16, RANK, 256), BF16),
            pltpu.VMEM((64, 128), F32),
            pltpu.VMEM((8, RANK, 128), F32),
            pltpu.VMEM((8, RANK, 128), F32),
            pltpu.VMEM((WIDTH, 768), BF16),
            pltpu.VMEM((INNER, WIDTH), BF16),
            pltpu.VMEM((2, 2, 512, WIDTH), BF16),
            pltpu.VMEM((2, 2, 1024, 768), BF16),
            pltpu.VMEM((2, 2, 2, RANK, 512), BF16),
            pltpu.VMEM((4, 512, 256), BF16),
            pltpu.VMEM((8, 4, 64, 256), BF16),
            pltpu.VMEM((8, 64, 128), BF16),
            pltpu.VMEM((64, 128), BF16),
            pltpu.VMEM((RANK, INNER), BF16),
            pltpu.VMEM((RANK, 256), BF16),
            pltpu.VMEM((RANK, 768), BF16),
            pltpu.VMEM((2, 2, 64, INNER), BF16),
            pltpu.VMEM((2, 2, 512, 256), BF16),
            pltpu.VMEM((256, WIDTH), BF16),
            pltpu.VMEM((1024, 256), BF16),
            pltpu.VMEM((2, RANK, 1024), F32),
            pltpu.VMEM((2, 16, RANK, 128), F32),
            pltpu.VMEM((2, 16, RANK, 128), F32),
            pltpu.VMEM((RANK, WIDTH), F32),
            pltpu.VMEM((RANK, WIDTH), F32),
            dma((4, 9)), dma((4, 9)),
            dma((4, 5)), dma((4, 5)),
            dma((2, 8)), dma((2, 8)),
            dma((8,)), dma((8,)),
            dma((4, 16)), dma((4, 16)),
            dma((2, 16)), dma((2, 16)),
            dma((2, 3)), dma((2, 3)),
            dma((16,)),
            dma((2, 16)), dma((2, 16)),
            dma, dma,
            dma((8,)), dma((8,)),
            dma((3,)),
        ],
        compiler_params=pltpu.CompilerParams(
            collective_id=0, has_side_effects=True, vmem_limit_bytes=58 * 1024 * 1024
        ),
        name="rollout",
    )(
        perturbed_codes,
        random_draws,
        relative_rewards,
        rescaling_gains,
        triple_projector,
        emission_projector,
        payload_bypass_reducer.T,
        payload_bypass_lift,
        outlet_bypass_reducer.T,
        outlet_bypass_lift,
    )
    wide, narrow = WIDTH // 128, INNER // 128
    ends = (0, wide, 2 * wide, 2 * wide + narrow, 2 * wide + 2 * narrow)
    gav, gup, gbv, gred = (sums[a:b] for a, b in zip(ends, ends[1:]))
    return (final, gav, gbv.T, gred, gup.T)


def solution(mesh):
    placed = (
        P("fsdp", "seq", None),
        P(None, "fsdp", "seq", None),
        P("fsdp"),
        P(),
        P(None, "seq"),
        P(),
        P(),
        P(),
        P(),
        P(),
    )
    return jax.shard_map(
        per_device,
        mesh=mesh,
        in_specs=placed,
        out_specs=(
            P("fsdp", "seq", None),
            P(("seq", "fsdp"), None),
            P(None, ("seq", "fsdp")),
            P(("seq", "fsdp"), None),
            P(None, ("seq", "fsdp")),
        ),
        check_vma=False,
    )
```
